256 devices in a mesh: seq: 16 (over x, y_lo, core), wt: 16 (over y_hi, z).
Axes of the slice: x: 4, y: 4 (y_hi: 2, y_lo: 2; y = y_hi * 2 + y_lo), z: 8, core: 2. Of those that a mesh axis runs over, the one named last changes fastest.
Arguments:
- hidden_states: bfloat16 [4096, 8192], P('seq'), may hold values from -32 to 32
- norm_gain: bfloat16 [8192], replicated, may hold values from 0.099609375 to 1.8984375
- query_weight: bfloat16 [8192, 8192], P('seq', 'wt')
- key_value_matrix: bfloat16 [8192, 2048], P('seq')
- output_weight: bfloat16 [8192, 8192], P('wt', 'seq'), may hold values from -0.0625 to 0.0625
Outputs:
- sublayer_out: bfloat16 [4096, 8192], P('seq', 'wt')
The draws below stay inside these ranges and needn't reach their ends.
All inputs are finite; a program needn't handle non-finite values.
Results may differ from the reference program's by a relative error of at most 0.0095.
Values may be sent and summed in bfloat16 or wider, within the bound.
A program may use at most 128 MiB of HBM per device.

```python
import math
import jax
import jax.numpy as jnp
from jax import lax

MODEL_WIDTH = 8192
QUERY_HEADS = 64
KEY_VALUE_HEADS = 8
HEAD_SIZE = 128
SEQUENCE_TOKENS = 4096
N_WT = 16


def shared_keys(key):
    base_column = jax.random.truncated_normal(jax.random.fold_in(key, 11), -5.0, 5.0, (MODEL_WIDTH, KEY_VALUE_HEADS, HEAD_SIZE), jnp.float32)
    return base_column * MODEL_WIDTH ** (-0.5)


def draw_hidden_states(key, part):
    key = jax.random.fold_in(key, 3)
    row_key, col_key, base_key = jax.random.split(key, 3)
    row_scale = jnp.exp(jax.random.uniform(row_key, (SEQUENCE_TOKENS, 1), jnp.float32, math.log(0.4), math.log(4.0)))
    col_scale = jnp.exp(jax.random.uniform(col_key, (1, MODEL_WIDTH), jnp.float32, math.log(0.5), math.log(2.0)))
    base_column = jax.random.truncated_normal(base_key, -4.0, 4.0, (SEQUENCE_TOKENS, MODEL_WIDTH), jnp.float32)
    return (base_column * row_scale * col_scale).astype(jnp.bfloat16)


def draw_query_weight(key, part):
    key = jax.random.fold_in(key, 5)
    noise_key = jax.random.fold_in(key, 0)
    noise = jax.random.truncated_normal(noise_key, -5.0, 5.0, (MODEL_WIDTH, QUERY_HEADS, HEAD_SIZE), jnp.float32) * MODEL_WIDTH ** (-0.5)
    result = noise
    return result.reshape(MODEL_WIDTH, QUERY_HEADS * HEAD_SIZE).astype(jnp.bfloat16)


def draw_key_value_matrix(key, part):
    shared_heads = shared_keys(key)
    key = jax.random.fold_in(key, 7)
    value_columns = jax.random.truncated_normal(key, -5.0, 5.0, (MODEL_WIDTH, KEY_VALUE_HEADS, HEAD_SIZE), jnp.float32) * MODEL_WIDTH ** (-0.5)
    return jnp.stack([shared_heads, value_columns], axis=2).reshape(MODEL_WIDTH, KEY_VALUE_HEADS * 2 * HEAD_SIZE).astype(jnp.bfloat16)


def shard_levels(rng, extent, shards, least, largest):
    gain = 1.0
    for dim, blocks in shards:
        steps = jax.random.uniform(jax.random.fold_in(jax.random.fold_in(rng, 6), dim), (blocks,), jnp.float32, least / len(shards), largest / len(shards))
        gain = gain * jnp.repeat(jnp.exp(steps), extent[dim] // blocks).reshape((-1,) + (1,) * (len(extent) - 1 - dim))
    return gain


def centred(rng, dims, deviation, reach, pieces=(), kind=jnp.bfloat16):
    entries = deviation * jax.random.normal(rng, dims, jnp.float32)
    if pieces:
        entries = entries * shard_levels(rng, dims, pieces, -0.22, 0.18)
    return jnp.clip(entries, -reach, reach).astype(kind)


def setup_inputs(seed: int = 0) -> dict:
    key_list = jax.random.split(jax.random.key(seed), 6)
    hidden_states = draw_hidden_states(jax.random.fold_in(key_list[5], 71), 0)
    norm_gain = jnp.clip(1.0 + 0.18 * jax.random.normal(key_list[1], (MODEL_WIDTH,), jnp.float32), 0.099609375, 1.8984375).astype(jnp.bfloat16)
    query_weight = draw_query_weight(jax.random.fold_in(key_list[5], 71), 0)
    key_value_matrix = draw_key_value_matrix(jax.random.fold_in(key_list[5], 71), 0)
    output_weight = centred(key_list[4], (QUERY_HEADS * HEAD_SIZE, MODEL_WIDTH), (QUERY_HEADS * HEAD_SIZE) ** -0.5, 0.0625, ((0, 16), (1, 16)))
    return dict(hidden_states=hidden_states, norm_gain=norm_gain, query_weight=query_weight, key_value_matrix=key_value_matrix, output_weight=output_weight)


def rope_tables(count, offset):
    positions = jnp.arange(count, dtype=jnp.float32) + offset
    exponent = jnp.arange(HEAD_SIZE // 2, dtype=jnp.float32) * (2.0 / HEAD_SIZE)
    inverse = jnp.power(jnp.float32(500000.0), -exponent)
    angles = positions[:, None] * inverse[None, :]
    return (jnp.cos(angles), jnp.sin(angles))

def rotate_half(vectors, cosines, sines):
    half = vectors.shape[-1] // 2
    first = vectors[..., :half]
    second = vectors[..., half:]
    cos_wide = cosines[:, None, :]
    sin_wide = sines[:, None, :]
    return jnp.concatenate([first * cos_wide - second * sin_wide, second * cos_wide + first * sin_wide], axis=-1)

def reference(hidden_states, norm_gain, query_weight, key_value_matrix, output_weight):
    states = hidden_states.astype(jnp.float32)
    inverse_rms = lax.rsqrt(lax.optimization_barrier(jnp.mean(states * states, axis=1, keepdims=True)) + 1e-05)
    normalized_input = (states * inverse_rms * norm_gain.astype(jnp.float32)[None, :]).astype(jnp.bfloat16)
    cosines, sines = rope_tables(SEQUENCE_TOKENS, 0.0)
    query_raw = jnp.dot(normalized_input, query_weight, preferred_element_type=jnp.float32).reshape(SEQUENCE_TOKENS, QUERY_HEADS, HEAD_SIZE)
    queries = rotate_half(query_raw, cosines, sines).astype(jnp.bfloat16)
    projected_rows = jnp.dot(normalized_input, key_value_matrix, preferred_element_type=jnp.float32).reshape(SEQUENCE_TOKENS, KEY_VALUE_HEADS, 2, HEAD_SIZE)
    keys = rotate_half(projected_rows[:, :, 0], cosines, sines).astype(jnp.bfloat16)
    values = projected_rows[:, :, 1].astype(jnp.bfloat16)
    positions = jnp.arange(SEQUENCE_TOKENS, dtype=jnp.int32)
    allowed = positions[None, :] <= positions[:, None]
    queries_per_group = QUERY_HEADS // KEY_VALUE_HEADS
    score_scale = 1.0 / math.sqrt(HEAD_SIZE)

    def one_head(head):
        query_head = lax.dynamic_index_in_dim(queries, head, 1, keepdims=False)
        key_head = lax.dynamic_index_in_dim(keys, head // queries_per_group, 1, keepdims=False)
        value_head = lax.dynamic_index_in_dim(values, head // queries_per_group, 1, keepdims=False)
        scores = jnp.dot(query_head, key_head.T, preferred_element_type=jnp.float32) * score_scale
        scores = jnp.where(allowed, scores, -1e+30)
        highest = lax.optimization_barrier(jnp.max(scores, axis=1, keepdims=True))
        weights = jnp.where(allowed, jnp.exp(scores - highest), 0.0)
        totals = lax.optimization_barrier(jnp.sum(weights, axis=1, keepdims=True))
        mixed = jnp.dot(weights, value_head.astype(jnp.float32), precision=lax.Precision.HIGHEST)
        return (mixed / totals).astype(jnp.bfloat16)
    heads = lax.map(one_head, jnp.arange(QUERY_HEADS, dtype=jnp.int32))
    attention = jnp.transpose(heads, (1, 0, 2)).reshape(SEQUENCE_TOKENS, QUERY_HEADS * HEAD_SIZE)
    panel_width = QUERY_HEADS * HEAD_SIZE // N_WT
    grouped = jnp.transpose(attention.reshape(SEQUENCE_TOKENS, N_WT, panel_width), (1, 0, 2))
    panels = output_weight.reshape(N_WT, panel_width, MODEL_WIDTH)

    def accumulate(running, pair):
        term = jnp.dot(pair[0], pair[1], preferred_element_type=jnp.float32)
        rounded = lax.optimization_barrier(term.astype(jnp.bfloat16))
        return (running + rounded.astype(jnp.float32), None)
    summed, _ = lax.scan(accumulate, jnp.zeros((SEQUENCE_TOKENS, MODEL_WIDTH), jnp.float32), (grouped, panels))
    return (states + summed).astype(jnp.bfloat16)
```

```python
import math

import jax
import jax.numpy as jnp
import numpy as np
from jax import lax
from jax.experimental import pallas as pl
from jax.experimental.pallas import tpu as pltpu
from jax.sharding import PartitionSpec as P

MESH = pl.DeviceIdType.MESH
HEAD = 128
ROWS = 256
SHARDS = 16
BLOCK = 512
HEADS_HERE = 4
SCORE_LOG2 = math.log2(math.e) / math.sqrt(HEAD)
KV_WEIGHT, QUERY, OUTPUT, KEYS = 0, 1, 2, 3
f32 = jnp.float32
bf16 = jnp.bfloat16


def rope_constants():
    inverse = 500000.0 ** (-np.arange(HEAD // 2) * 2.0 / HEAD)
    wide = np.concatenate([inverse, inverse])
    sign = np.concatenate([-np.ones(HEAD // 2), np.ones(HEAD // 2)])
    inner = np.arange(ROWS)[:, None] * wide[None, :]
    outer = (np.arange(SHARDS) * ROWS)[:, None] * wide[None, :]
    tables = (np.cos(inner), np.sin(inner) * sign, np.cos(outer), np.sin(outer) * sign)
    return [t.astype(np.float32) for t in tables]


def body(
    hidden_ref, gain_ref, wq_ref, wkv_ref, wo_ref, cr_ref, sr_ref, cb_ref, sb_ref,
    out_ref,
    hid, normed, wkv, wq, wo, kv, qacc, qrot, macc, oacc, attn,
    snd4, rcv4, snd, rcv, ysnd, yrcv, total,
    gsend, grecv, rsend, rrecv, xsend, xrecv, lsem,
):
    s = lax.axis_index("seq")
    w = lax.axis_index("wt")
    x, yl, core = lax.div(s, 4), lax.rem(lax.div(s, 2), 2), lax.rem(s, 2)
    yh, z = lax.div(w, 8), lax.rem(w, 8)
    xp, xm, xo = lax.rem(x + 1, 4), lax.rem(x + 3, 4), lax.rem(x + 2, 4)
    yp, sib_core = 1 - yl, 1 - core
    par = lax.rem(z, 2)
    chip = lax.div(s, 2)

    def sid(xi, yi, ci):
        return (xi * 2 + yi) * 2 + ci

    def wid(yi, zi):
        return yi * 8 + zi

    to_xp, to_xm = (sid(xp, yl, core), w), (sid(xm, yl, core), w)
    to_y, to_sib = (sid(x, yp, core), w), (sid(x, yl, sib_core), w)
    to_zp, to_zm = (s, wid(yh, lax.rem(z + 1, 8))), (s, wid(yh, lax.rem(z + 7, 8)))
    to_yh = (s, wid(1 - yh, z))
    to_pair = (s, wid(yh, z + 1 - 2 * par))

    barrier = pltpu.get_barrier_semaphore()
    for peer in (to_xp, to_xm, to_y, to_sib, to_zp, to_zm, to_yh):
        pl.semaphore_signal(barrier, inc=1, device_id=peer, device_id_type=MESH)

    first = pltpu.make_async_copy(
        wkv_ref.at[:, pl.ds(pl.multiple_of(w * HEAD, HEAD), HEAD)], wkv.at[s], lsem.at[0]
    )
    load_hidden = pltpu.make_async_copy(hidden_ref, hid, lsem.at[1])
    load_q = pltpu.make_async_copy(wq_ref, wq.at[s], lsem.at[2])
    load_o = pltpu.make_async_copy(wo_ref, wo.at[s], lsem.at[3])
    first.start()
    load_hidden.start()
    load_q.start()
    load_o.start()
    pl.semaphore_wait(barrier, 7)

    stores = {KV_WEIGHT: wkv, QUERY: wq, OUTPUT: wo}

    def slot(k, shard, half=None):
        if k == KEYS:
            rows = pl.ds(pl.multiple_of(shard * ROWS, ROWS), ROWS)
            return kv.at[:, rows] if half is None else kv.at[half, rows]
        if half is None:
            return stores[k].at[shard]
        return stores[k].at[shard, pl.ds(half * 256, 256)]

    started = []

    def send(k, label, source, place, peer):
        copy = pltpu.make_async_remote_copy(
            src_ref=source, dst_ref=place, send_sem=gsend.at[k, label], recv_sem=grecv.at[k, label],
            device_id=peer, device_id_type=MESH,
        )
        copy.start()
        started.append(copy)

    def forward(k, label, shard, peer, half=None):
        send(k, label, slot(k, shard, half), slot(k, shard, half), peer)

    def arrive(k, label, shard, half=None):
        place = slot(k, shard, half)
        pltpu.make_async_remote_copy(
            src_ref=place, dst_ref=place, send_sem=gsend.at[k, label], recv_sem=grecv.at[k, label],
            device_id=to_sib, device_id_type=MESH,
        ).wait_recv()

    chips = [(x, yl), (x, yp), (xm, yl), (xp, yl), (xm, yp), (xp, yp), (xo, yl), (xo, yp)]
    mine = [sid(a, b, core) for a, b in chips]
    theirs = [sid(a, b, sib_core) for a, b in chips]
    sib_label = [3, 9, 10, 11, 12, 13, 14, 15]

    def own_sends(k, source):
        for label, peer in ((0, to_xp), (1, to_xm), (2, to_y), (3, to_sib)):
            send(k, label, source, slot(k, s), peer)

    def near(k):
        arrive(k, 0, mine[2])
        forward(k, 6, mine[2], to_xp, 0)
        arrive(k, 1, mine[3])
        forward(k, 7, mine[3], to_xm, 1)
        arrive(k, 2, mine[1])
        forward(k, 4, mine[1], to_xp)
        forward(k, 5, mine[1], to_xm)
        for p in (1, 2, 3):
            forward(k, sib_label[p], mine[p], to_sib)

    def middle(k):
        arrive(k, 6, mine[6], 0)
        arrive(k, 7, mine[6], 1)
        forward(k, 8, mine[6], to_y)
        forward(k, sib_label[6], mine[6], to_sib)
        arrive(k, 4, mine[4])
        forward(k, sib_label[4], mine[4], to_sib)
        arrive(k, 5, mine[5])
        forward(k, sib_label[5], mine[5], to_sib)

    def far(k):
        arrive(k, 8, mine[7])
        forward(k, sib_label[7], mine[7], to_sib)

    def from_sib(k, p):
        arrive(k, sib_label[p], theirs[p])

    first.wait()
    own_sends(KV_WEIGHT, wkv.at[s])
    own_sends(QUERY, wq_ref)

    load_hidden.wait()

    def square(i, acc):
        block = hid[:, pl.ds(pl.multiple_of(i * BLOCK, BLOCK), BLOCK)].astype(f32)
        block = block * block
        return acc + (block[:, :128] + block[:, 128:256]) + (block[:, 256:384] + block[:, 384:])

    squares = lax.fori_loop(0, SHARDS, square, jnp.zeros((ROWS, 128), f32))
    inverse = lax.rsqrt(jnp.sum(squares, axis=1, keepdims=True) * (1.0 / 8192.0) + 1e-05)

    near(KV_WEIGHT)

    def scale(i, _):
        columns = pl.ds(pl.multiple_of(i * BLOCK, BLOCK), BLOCK)
        block = hid[:, columns].astype(f32) * inverse * gain_ref[:, columns].astype(f32)
        normed[i] = block.astype(bf16)
        return 0

    lax.fori_loop(0, SHARDS, scale, 0)
    middle(KV_WEIGHT)
    far(KV_WEIGHT)

    for p in range(8):
        from_sib(KV_WEIGHT, p)

    def project(i, acc):
        return acc + jnp.dot(normed[i], wkv[i], preferred_element_type=f32)

    raw = lax.fori_loop(0, SHARDS, project, jnp.zeros((ROWS, HEAD), f32))
    near(QUERY)
    base = pl.ds(s, 1)
    cosines = cb_ref[base, :] * cr_ref[...] - sb_ref[base, :] * sr_ref[...]
    sines = sb_ref[base, :] * cr_ref[...] + cb_ref[base, :] * sr_ref[...]

    def rotate(u):
        return u * cosines + pltpu.roll(u, HEAD // 2, 1) * sines

    rows_here = pl.ds(pl.multiple_of(s * ROWS, ROWS), ROWS)
    is_value = (lax.broadcasted_iota(jnp.int32, (ROWS, HEAD), 0) * 0 + par) == 1
    kv[par, rows_here] = jnp.where(is_value, raw, rotate(raw)).astype(bf16)
    pair = pltpu.make_async_remote_copy(
        src_ref=kv.at[par, rows_here], dst_ref=kv.at[par, rows_here], send_sem=xsend.at[0], recv_sem=xrecv.at[0],
        device_id=to_pair, device_id_type=MESH,
    )
    pair.start()
    started.append(pair)
    load_q.wait()

    def accumulate(shard, start=False):
        term = jnp.dot(normed[shard], wq[shard], preferred_element_type=f32)
        qacc[...] = term if start else qacc[...] + term

    accumulate(mine[0], True)
    pltpu.make_async_remote_copy(
        src_ref=kv.at[1 - par, rows_here], dst_ref=kv.at[1 - par, rows_here], send_sem=xsend.at[0],
        recv_sem=xrecv.at[0], device_id=to_pair, device_id_type=MESH,
    ).wait_recv()
    own_sends(KEYS, slot(KEYS, s))
    for p in (1, 2, 3):
        accumulate(mine[p])
    near(KEYS)
    own_sends(OUTPUT, wo_ref)
    for p in (0, 1, 2, 3):
        from_sib(QUERY, p)
        accumulate(theirs[p])
    middle(QUERY)
    middle(KEYS)
    for p in (4, 5, 6):
        accumulate(mine[p])
    far(KEYS)
    far(QUERY)
    for p in (4, 5, 6):
        from_sib(QUERY, p)
        accumulate(theirs[p])
    accumulate(mine[7])
    from_sib(QUERY, 7)
    accumulate(theirs[7])
    for h in range(HEADS_HERE):
        qrot[h] = rotate(qacc[:, h * HEAD : (h + 1) * HEAD]).astype(bf16)
    for p in range(8):
        from_sib(KEYS, p)

    ones = jnp.ones((BLOCK, HEAD), bf16)

    def scores_of(h, block):
        rows = pl.ds(pl.multiple_of(block * BLOCK, BLOCK), BLOCK)
        return lax.dot_general(
            qrot[h], kv[0, rows], (((1,), (1,)), ((), ())), preferred_element_type=f32
        )

    def values_of(block):
        rows = pl.ds(pl.multiple_of(block * BLOCK, BLOCK), BLOCK)
        return jnp.concatenate([kv[1, rows], ones], axis=1)

    query_at = lax.broadcasted_iota(jnp.int32, (ROWS, BLOCK), 0) + core * ROWS
    allowed = lax.broadcasted_iota(jnp.int32, (ROWS, BLOCK), 1) <= query_at
    for h in range(HEADS_HERE):
        scores = jnp.where(allowed, scores_of(h, chip), -1e30)
        high = jnp.max(scores, axis=1, keepdims=True)
        weights = jnp.exp2((scores - high) * SCORE_LOG2).astype(bf16)
        oacc[h] = jnp.dot(weights, values_of(chip), preferred_element_type=f32)
        macc[h] = jnp.broadcast_to(high, (ROWS, HEAD))

    def attend(block, _):
        values = values_of(block)
        for h in range(HEADS_HERE):
            scores = scores_of(h, block)
            before = macc[h][:, :1]
            high = jnp.maximum(before, jnp.max(scores, axis=1, keepdims=True))
            weights = jnp.exp2((scores - high) * SCORE_LOG2).astype(bf16)
            keep = jnp.exp2((before - high) * SCORE_LOG2)
            oacc[h] = oacc[h] * keep + jnp.dot(weights, values, preferred_element_type=f32)
            macc[h] = jnp.broadcast_to(high, (ROWS, HEAD))
        return 0

    near(OUTPUT)
    lax.fori_loop(0, jnp.minimum(chip, 4), attend, 0)
    middle(OUTPUT)
    lax.fori_loop(4, jnp.maximum(chip, 4), attend, 0)
    for h in range(HEADS_HERE):
        attn[:, h * HEAD : (h + 1) * HEAD] = (oacc[h][:, :HEAD] / oacc[h][:, HEAD:]).astype(bf16)
    far(OUTPUT)
    load_o.wait()
    for p in range(8):
        from_sib(OUTPUT, p)

    def partial(yi, zi):
        return jnp.dot(attn[...], wo[wid(yi, zi)], preferred_element_type=f32)

    order = (1 - yh, yh)

    def hop(label, source, place, peer):
        copy = pltpu.make_async_remote_copy(
            src_ref=source, dst_ref=place, send_sem=rsend.at[label], recv_sem=rrecv.at[label],
            device_id=peer, device_id_type=MESH,
        )
        copy.start()
        started.append(copy)

    def landed(label, place):
        pltpu.make_async_remote_copy(
            src_ref=place, dst_ref=place, send_sem=rsend.at[label], recv_sem=rrecv.at[label],
            device_id=to_sib, device_id_type=MESH,
        ).wait_recv()

    halves = (pl.ds(0, 128), pl.ds(128, 128))
    ways = (to_zp, to_zm)
    for j in range(2):
        snd4[j] = partial(order[j], lax.rem(z + 4, 8)).astype(bf16)
        for way in range(2):
            hop(way * 2 + j, snd4.at[j, halves[way]], rcv4.at[j, halves[way]], ways[way])
    for d in (3, 2, 1):
        for j in range(2):
            for way in range(2):
                at = lax.rem(z + d, 8) if way == 0 else lax.rem(z + 8 - d, 8)
                term = partial(order[j], at)
                if d == 3:
                    landed(way * 2 + j, rcv4.at[j, halves[way]])
                    got = rcv4[j, halves[way]].astype(f32)
                    if way == 0:
                        snd[d - 1, way, j, :128] = (term[:128] + got).astype(bf16)
                        snd[d - 1, way, j, 128:] = term[128:].astype(bf16)
                    else:
                        snd[d - 1, way, j, :128] = term[:128].astype(bf16)
                        snd[d - 1, way, j, 128:] = (term[128:] + got).astype(bf16)
                else:
                    landed((4 - d - 1) * 4 + way * 2 + j, rcv.at[d, way, j])
                    snd[d - 1, way, j] = (term + rcv[d, way, j].astype(f32)).astype(bf16)
                hop((4 - d) * 4 + way * 2 + j, snd.at[d - 1, way, j], rcv.at[d - 1, way, j], ways[way])
    for j in range(2):
        term = partial(order[j], z)
        for way in range(2):
            landed(12 + way * 2 + j, rcv.at[0, way, j])
            term = term + rcv[0, way, j].astype(f32)
        if j == 0:
            ysnd[...] = term.astype(bf16)
            hop(16, ysnd, yrcv, to_yh)
        else:
            columns = pl.ds(pl.multiple_of(w * BLOCK, BLOCK), BLOCK)
            total[...] = term + hid[:, columns].astype(f32)
    landed(16, yrcv)
    out_ref[...] = (total[...] + yrcv[...].astype(f32)).astype(bf16)
    for copy in started:
        copy.wait_send()


def local(hidden_states, norm_gain, query_weight, key_value_matrix, output_weight):
    tables = [jnp.asarray(t) for t in rope_constants()]
    anywhere = pl.BlockSpec(memory_space=pl.ANY)
    inside = pl.BlockSpec(memory_space=pltpu.VMEM)
    dma = pltpu.SemaphoreType.DMA
    return pl.pallas_call(
        body,
        out_shape=jax.ShapeDtypeStruct((ROWS, BLOCK), bf16),
        in_specs=[anywhere, inside, anywhere, anywhere, anywhere] + [inside] * 4,
        out_specs=inside,
        scratch_shapes=[
            pltpu.VMEM((ROWS, 8192), bf16),
            pltpu.VMEM((SHARDS, ROWS, BLOCK), bf16),
            pltpu.VMEM((SHARDS, BLOCK, HEAD), bf16),
            pltpu.VMEM((SHARDS, BLOCK, BLOCK), bf16),
            pltpu.VMEM((SHARDS, BLOCK, BLOCK), bf16),
            pltpu.VMEM((2, SHARDS * ROWS, HEAD), bf16),
            pltpu.VMEM((ROWS, BLOCK), f32),
            pltpu.VMEM((HEADS_HERE, ROWS, HEAD), bf16),
            pltpu.VMEM((HEADS_HERE, ROWS, HEAD), f32),
            pltpu.VMEM((HEADS_HERE, ROWS, 2 * HEAD), f32),
            pltpu.VMEM((ROWS, BLOCK), bf16),
            pltpu.VMEM((2, ROWS, BLOCK), bf16),
            pltpu.VMEM((2, ROWS, BLOCK), bf16),
            pltpu.VMEM((3, 2, 2, ROWS, BLOCK), bf16),
            pltpu.VMEM((3, 2, 2, ROWS, BLOCK), bf16),
            pltpu.VMEM((ROWS, BLOCK), bf16),
            pltpu.VMEM((ROWS, BLOCK), bf16),
            pltpu.VMEM((ROWS, BLOCK), f32),
            dma((4, 16)),
            dma((4, 16)),
            dma((17,)),
            dma((17,)),
            dma((1,)),
            dma((1,)),
            dma((4,)),
        ],
        compiler_params=pltpu.CompilerParams(
            collective_id=0, has_side_effects=True, vmem_limit_bytes=56 * 1024 * 1024
        ),
    )(hidden_states, norm_gain.reshape(1, -1), query_weight, key_value_matrix, output_weight, *tables)


def solution(mesh):
    in_specs = (P("seq", None), P(), P("seq", "wt"), P("seq", None), P("wt", "seq"))
    return jax.shard_map(local, mesh=mesh, in_specs=in_specs, out_specs=P("seq", "wt"), check_vma=False)
```

```python
import math

import jax
import jax.numpy as jnp
import numpy as np
from jax import lax
from jax.experimental import pallas as pl
from jax.experimental.pallas import tpu as pltpu
from jax.sharding import PartitionSpec as P

MESH = pl.DeviceIdType.MESH
HEAD = 128
ROWS = 256
SHARDS = 16
BLOCK = 512
HEADS_HERE = 4
SCORE_LOG2 = math.log2(math.e) / math.sqrt(HEAD)
KV_WEIGHT, QUERY, OUTPUT, KEYS = 0, 1, 2, 3
f32 = jnp.float32
bf16 = jnp.bfloat16


def rope_constants():
    inverse = 500000.0 ** (-np.arange(HEAD // 2) * 2.0 / HEAD)
    wide = np.concatenate([inverse, inverse])
    sign = np.concatenate([-np.ones(HEAD // 2), np.ones(HEAD // 2)])
    inner = np.arange(ROWS)[:, None] * wide[None, :]
    outer = (np.arange(SHARDS) * ROWS)[:, None] * wide[None, :]
    tables = (np.cos(inner), np.sin(inner) * sign, np.cos(outer), np.sin(outer) * sign)
    return [t.astype(np.float32) for t in tables]


def body(
    hidden_ref, gain_ref, wq_ref, wkv_ref, wo_ref, cr_ref, sr_ref, cb_ref, sb_ref,
    out_ref,
    hid, normed, wkv, wq, wo, kv, qacc, qrot, macc, oacc, heads, tacc, ysnd, yrcv,
    gsend, grecv, rsend, rrecv, dsend, drecv, xsend, xrecv, lsem,
):
    s = lax.axis_index("seq")
    w = lax.axis_index("wt")
    x, yl, core = lax.div(s, 4), lax.rem(lax.div(s, 2), 2), lax.rem(s, 2)
    yh, z = lax.div(w, 8), lax.rem(w, 8)
    xp, xm, xo = lax.rem(x + 1, 4), lax.rem(x + 3, 4), lax.rem(x + 2, 4)
    yp, sib_core = 1 - yl, 1 - core
    par = lax.rem(z, 2)
    chip = lax.div(s, 2)

    def sid(xi, yi, ci):
        return (xi * 2 + yi) * 2 + ci

    def wid(yi, zi):
        return yi * 8 + zi

    to_xp, to_xm = (sid(xp, yl, core), w), (sid(xm, yl, core), w)
    to_y, to_sib = (sid(x, yp, core), w), (sid(x, yl, sib_core), w)
    to_zp, to_zm = (s, wid(yh, lax.rem(z + 1, 8))), (s, wid(yh, lax.rem(z + 7, 8)))
    to_yh = (s, wid(1 - yh, z))
    to_pair = (s, wid(yh, z + 1 - 2 * par))

    barrier = pltpu.get_barrier_semaphore()
    for peer in (to_xp, to_xm, to_y, to_sib, to_zp, to_zm, to_yh):
        pl.semaphore_signal(barrier, inc=1, device_id=peer, device_id_type=MESH)
    keeps_piece = lax.rem(s, 8) == z
    deal_label = lax.div(s, 8) * 8 + z

    def greet(label):
        dealer = (z + 8 * lax.div(label, 8), wid(yh, lax.rem(label, 8)))
        pl.semaphore_signal(barrier, inc=1, device_id=dealer, device_id_type=MESH)

    for i in range(1, SHARDS):
        greet(lax.rem(deal_label + i, SHARDS))

    @pl.when(jnp.logical_not(keeps_piece))
    def _():
        greet(deal_label)

    first = pltpu.make_async_copy(
        wkv_ref.at[:, pl.ds(pl.multiple_of(w * HEAD, HEAD), HEAD)], wkv.at[s], lsem.at[0]
    )
    load_hidden = pltpu.make_async_copy(hidden_ref, hid, lsem.at[1])
    load_q = pltpu.make_async_copy(wq_ref, wq.at[s], lsem.at[2])
    first.start()
    load_hidden.start()
    load_q.start()
    pl.semaphore_wait(barrier, 7 + SHARDS - jnp.where(keeps_piece, 1, 0))

    stores = {KV_WEIGHT: wkv, QUERY: wq, OUTPUT: wo}

    def slot(k, shard, half=None):
        if k == KEYS:
            rows = pl.ds(pl.multiple_of(shard * ROWS, ROWS), ROWS)
            return kv.at[:, rows] if half is None else kv.at[half, rows]
        if half is None:
            return stores[k].at[shard]
        if k == OUTPUT:
            return wo.at[shard, half]
        return stores[k].at[shard, pl.ds(half * 256, 256)]

    started = []

    def send(k, label, source, place, peer):
        copy = pltpu.make_async_remote_copy(
            src_ref=source, dst_ref=place, send_sem=gsend.at[k, label], recv_sem=grecv.at[k, label],
            device_id=peer, device_id_type=MESH,
        )
        copy.start()
        started.append(copy)

    def forward(k, label, shard, peer, half=None):
        send(k, label, slot(k, shard, half), slot(k, shard, half), peer)

    def arrive(k, label, shard, half=None):
        place = slot(k, shard, half)
        pltpu.make_async_remote_copy(
            src_ref=place, dst_ref=place, send_sem=gsend.at[k, label], recv_sem=grecv.at[k, label],
            device_id=to_sib, device_id_type=MESH,
        ).wait_recv()

    chips = [(x, yl), (x, yp), (xm, yl), (xp, yl), (xm, yp), (xp, yp), (xo, yl), (xo, yp)]
    mine = [sid(a, b, core) for a, b in chips]
    theirs = [sid(a, b, sib_core) for a, b in chips]
    sib_label = [3, 9, 10, 11, 12, 13, 14, 15]

    def own_sends(k, source):
        for label, peer in ((0, to_xp), (1, to_xm), (2, to_y), (3, to_sib)):
            send(k, label, source, slot(k, s), peer)

    def near(k):
        arrive(k, 0, mine[2])
        forward(k, 6, mine[2], to_xp, 0)
        arrive(k, 1, mine[3])
        forward(k, 7, mine[3], to_xm, 1)
        arrive(k, 2, mine[1])
        forward(k, 4, mine[1], to_xp)
        forward(k, 5, mine[1], to_xm)
        for p in (1, 2, 3):
            forward(k, sib_label[p], mine[p], to_sib)

    def middle(k):
        arrive(k, 6, mine[6], 0)
        arrive(k, 7, mine[6], 1)
        forward(k, 8, mine[6], to_y)
        forward(k, sib_label[6], mine[6], to_sib)
        arrive(k, 4, mine[4])
        forward(k, sib_label[4], mine[4], to_sib)
        arrive(k, 5, mine[5])
        forward(k, sib_label[5], mine[5], to_sib)

    def far(k):
        arrive(k, 8, mine[7])
        forward(k, sib_label[7], mine[7], to_sib)

    def from_sib(k, p):
        arrive(k, sib_label[p], theirs[p])

    first.wait()
    own_sends(KV_WEIGHT, wkv.at[s])
    own_sends(QUERY, wq_ref)

    def piece(p):
        return wo_ref.at[
            pl.ds(pl.multiple_of(lax.div(p, 4) * HEAD, HEAD), HEAD), pl.ds(pl.multiple_of(lax.rem(p, 4) * HEAD, HEAD), HEAD)
        ]

    def deal(i):
        p = lax.rem(s + i, SHARDS)
        return pltpu.make_async_remote_copy(
            src_ref=piece(p), dst_ref=wo.at[p, lax.div(s, 8), z], send_sem=dsend.at[i], recv_sem=drecv.at[deal_label],
            device_id=(p, wid(yh, lax.rem(s, 8))), device_id_type=MESH,
        )

    kept = pltpu.make_async_copy(piece(s), wo.at[s, lax.div(s, 8), z], lsem.at[3])
    for i in range(1, SHARDS):
        deal(i).start()

    @pl.when(keeps_piece)
    def _():
        kept.start()

    @pl.when(jnp.logical_not(keeps_piece))
    def _():
        deal(0).start()

    def dealt(label):
        place = wo.at[s, lax.div(label, 8), lax.rem(label, 8)]
        pltpu.make_async_remote_copy(
            src_ref=place, dst_ref=place, send_sem=dsend.at[0], recv_sem=drecv.at[label], device_id=to_sib,
            device_id_type=MESH,
        ).wait_recv()

    def all_dealt():
        for i in range(1, SHARDS):
            dealt(lax.rem(deal_label + i, SHARDS))

        @pl.when(keeps_piece)
        def _():
            kept.wait()

        @pl.when(jnp.logical_not(keeps_piece))
        def _():
            dealt(deal_label)

    load_hidden.wait()

    def square(i, acc):
        block = hid[:, pl.ds(pl.multiple_of(i * BLOCK, BLOCK), BLOCK)].astype(f32)
        block = block * block
        return acc + (block[:, :128] + block[:, 128:256]) + (block[:, 256:384] + block[:, 384:])

    squares = lax.fori_loop(0, SHARDS, square, jnp.zeros((ROWS, 128), f32))
    inverse = lax.rsqrt(jnp.sum(squares, axis=1, keepdims=True) * (1.0 / 8192.0) + 1e-05)

    near(KV_WEIGHT)

    def scale(i, _):
        columns = pl.ds(pl.multiple_of(i * BLOCK, BLOCK), BLOCK)
        block = hid[:, columns].astype(f32) * inverse * gain_ref[:, columns].astype(f32)
        normed[i] = block.astype(bf16)
        return 0

    lax.fori_loop(0, SHARDS, scale, 0)
    middle(KV_WEIGHT)
    far(KV_WEIGHT)

    for p in range(8):
        from_sib(KV_WEIGHT, p)

    def project(i, acc):
        return acc + jnp.dot(normed[i], wkv[i], preferred_element_type=f32)

    raw = lax.fori_loop(0, SHARDS, project, jnp.zeros((ROWS, HEAD), f32))
    near(QUERY)
    base = pl.ds(s, 1)
    cosines = cb_ref[base, :] * cr_ref[...] - sb_ref[base, :] * sr_ref[...]
    sines = sb_ref[base, :] * cr_ref[...] + cb_ref[base, :] * sr_ref[...]

    def rotate(u):
        return u * cosines + pltpu.roll(u, HEAD // 2, 1) * sines

    rows_here = pl.ds(pl.multiple_of(s * ROWS, ROWS), ROWS)
    is_value = (lax.broadcasted_iota(jnp.int32, (ROWS, HEAD), 0) * 0 + par) == 1
    kv[par, rows_here] = jnp.where(is_value, raw, rotate(raw)).astype(bf16)
    pair = pltpu.make_async_remote_copy(
        src_ref=kv.at[par, rows_here], dst_ref=kv.at[par, rows_here], send_sem=xsend.at[0], recv_sem=xrecv.at[0],
        device_id=to_pair, device_id_type=MESH,
    )
    pair.start()
    started.append(pair)
    load_q.wait()

    def accumulate(shard, start=False):
        term = jnp.dot(normed[shard], wq[shard], preferred_element_type=f32)
        qacc[...] = term if start else qacc[...] + term

    accumulate(mine[0], True)
    pltpu.make_async_remote_copy(
        src_ref=kv.at[1 - par, rows_here], dst_ref=kv.at[1 - par, rows_here], send_sem=xsend.at[0],
        recv_sem=xrecv.at[0], device_id=to_pair, device_id_type=MESH,
    ).wait_recv()
    own_sends(KEYS, slot(KEYS, s))
    for p in (1, 2, 3):
        accumulate(mine[p])
    near(KEYS)
    for p in (0, 1, 2, 3):
        from_sib(QUERY, p)
        accumulate(theirs[p])
    middle(QUERY)
    all_dealt()
    own_sends(OUTPUT, wo.at[s])
    middle(KEYS)
    for p in (4, 5, 6):
        accumulate(mine[p])
    far(KEYS)
    far(QUERY)
    for p in (4, 5, 6):
        from_sib(QUERY, p)
        accumulate(theirs[p])
    accumulate(mine[7])
    from_sib(QUERY, 7)
    accumulate(theirs[7])
    for h in range(HEADS_HERE):
        qrot[h] = rotate(qacc[:, h * HEAD : (h + 1) * HEAD]).astype(bf16)
    for p in range(8):
        from_sib(KEYS, p)

    ones = jnp.ones((BLOCK, HEAD), bf16)

    def scores_of(h, block):
        rows = pl.ds(pl.multiple_of(block * BLOCK, BLOCK), BLOCK)
        return lax.dot_general(
            qrot[h], kv[0, rows], (((1,), (1,)), ((), ())), preferred_element_type=f32
        )

    def values_of(block):
        rows = pl.ds(pl.multiple_of(block * BLOCK, BLOCK), BLOCK)
        return jnp.concatenate([kv[1, rows], ones], axis=1)

    query_at = lax.broadcasted_iota(jnp.int32, (ROWS, BLOCK), 0) + core * ROWS
    allowed = lax.broadcasted_iota(jnp.int32, (ROWS, BLOCK), 1) <= query_at
    def hop(label, source, place, peer):
        copy = pltpu.make_async_remote_copy(
            src_ref=source, dst_ref=place, send_sem=rsend.at[label], recv_sem=rrecv.at[label],
            device_id=peer, device_id_type=MESH,
        )
        copy.start()
        started.append(copy)

    def landed(label, place):
        pltpu.make_async_remote_copy(
            src_ref=place, dst_ref=place, send_sem=rsend.at[label], recv_sem=rrecv.at[label],
            device_id=to_sib, device_id_type=MESH,
        ).wait_recv()

    def zplace(source, h, half=None):
        return heads.at[source, h] if half is None else heads.at[source, h, pl.ds(half * 128, 128)]

    def zsource(way, d):
        return lax.rem(z + 8 - d, 8) if way == 0 else lax.rem(z + d, 8)

    def zsend(h, way, d):
        place = zplace(zsource(way, d - 1), h, way if d == 4 else None)
        hop((h * 2 + way) * 4 + d - 1, place, place, (to_zp, to_zm)[way])

    def zland(h, way, d):
        landed((h * 2 + way) * 4 + d - 1, zplace(zsource(way, d), h, way if d == 4 else None))

    def wave(turn):
        for d in (1, 2, 3, 4):
            h = turn - d
            if 0 <= h < HEADS_HERE:
                for way in range(2):
                    zland(h, way, d)
                    if d < 4:
                        zsend(h, way, d + 1)

    for h in range(HEADS_HERE):
        scores = jnp.where(allowed, scores_of(h, chip), -1e30)
        high = jnp.max(scores, axis=1, keepdims=True)
        weights = jnp.exp2((scores - high) * SCORE_LOG2).astype(bf16)
        oacc[...] = jnp.dot(weights, values_of(chip), preferred_element_type=f32)
        macc[...] = jnp.broadcast_to(high, (ROWS, HEAD))

        def attend(block, _, h=h):
            scores = scores_of(h, block)
            before = macc[:, :1]
            high = jnp.maximum(before, jnp.max(scores, axis=1, keepdims=True))
            weights = jnp.exp2((scores - high) * SCORE_LOG2).astype(bf16)
            keep = jnp.exp2((before - high) * SCORE_LOG2)
            oacc[...] = oacc[...] * keep + jnp.dot(weights, values_of(block), preferred_element_type=f32)
            macc[...] = jnp.broadcast_to(high, (ROWS, HEAD))
            return 0

        lax.fori_loop(0, chip, attend, 0)
        heads[z, h] = (oacc[:, :HEAD] / oacc[:, HEAD:]).astype(bf16)
        zsend(h, 0, 1)
        zsend(h, 1, 1)
        wave(h)
        if h == 1:
            near(OUTPUT)
        if h == 3:
            middle(OUTPUT)
    for turn in range(HEADS_HERE, HEADS_HERE + 4):
        wave(turn)
    far(OUTPUT)

    def columns_from(p, fresh):
        row, column = chips[p]
        place = row * 2 + column
        left = jnp.concatenate([heads[i, row] for i in range(8)], axis=1)
        for yi in range(2):
            right = jnp.concatenate(
                [wo[place * 2 + i, yi].reshape(8 * HEAD, HEAD) for i in range(2)], axis=1
            )
            term = jnp.dot(left, right, preferred_element_type=f32)
            tacc[yi, column] = term if fresh else tacc[yi, column] + term

    for n, (column, positions) in enumerate(((yl, (0, 2, 3, 6)), (yp, (1, 4, 5, 7)))):
        for p in positions:
            from_sib(OUTPUT, p)
            columns_from(p, p < 2)
        ysnd[column] = tacc[1 - yh, column].astype(bf16)
        hop(32 + n, ysnd.at[column], yrcv.at[column], to_yh)
    for n, column in enumerate((yl, yp)):
        landed(32 + n, yrcv.at[column])
        at = pl.ds(pl.multiple_of(column * 256, 256), 256)
        wide = pl.ds(pl.multiple_of(w * BLOCK + column * 256, 256), 256)
        out_ref[:, at] = (hid[:, wide].astype(f32) + tacc[yh, column] + yrcv[column].astype(f32)).astype(bf16)
    for copy in started:
        copy.wait_send()
    for i in range(1, SHARDS):
        deal(i).wait_send()

    @pl.when(jnp.logical_not(keeps_piece))
    def _():
        deal(0).wait_send()


def local(hidden_states, norm_gain, query_weight, key_value_matrix, output_weight):
    tables = [jnp.asarray(t) for t in rope_constants()]
    anywhere = pl.BlockSpec(memory_space=pl.ANY)
    inside = pl.BlockSpec(memory_space=pltpu.VMEM)
    dma = pltpu.SemaphoreType.DMA
    return pl.pallas_call(
        body,
        out_shape=jax.ShapeDtypeStruct((ROWS, BLOCK), bf16),
        in_specs=[anywhere, inside, anywhere, anywhere, anywhere] + [inside] * 4,
        out_specs=inside,
        scratch_shapes=[
            pltpu.VMEM((ROWS, 8192), bf16),
            pltpu.VMEM((SHARDS, ROWS, BLOCK), bf16),
            pltpu.VMEM((SHARDS, BLOCK, HEAD), bf16),
            pltpu.VMEM((SHARDS, BLOCK, BLOCK), bf16),
            pltpu.VMEM((SHARDS, 2, 8, HEAD, HEAD), bf16),
            pltpu.VMEM((2, SHARDS * ROWS, HEAD), bf16),
            pltpu.VMEM((ROWS, BLOCK), f32),
            pltpu.VMEM((HEADS_HERE, ROWS, HEAD), bf16),
            pltpu.VMEM((ROWS, HEAD), f32),
            pltpu.VMEM((ROWS, 2 * HEAD), f32),
            pltpu.VMEM((8, HEADS_HERE, ROWS, HEAD), bf16),
            pltpu.VMEM((2, 2, ROWS, 256), f32),
            pltpu.VMEM((2, ROWS, 256), bf16),
            pltpu.VMEM((2, ROWS, 256), bf16),
            dma((4, 16)),
            dma((4, 16)),
            dma((34,)),
            dma((34,)),
            dma((16,)),
            dma((16,)),
            dma((1,)),
            dma((1,)),
            dma((4,)),
        ],
        compiler_params=pltpu.CompilerParams(
            collective_id=0, has_side_effects=True, vmem_limit_bytes=56 * 1024 * 1024
        ),
    )(hidden_states, norm_gain.reshape(1, -1), query_weight, key_value_matrix, output_weight, *tables)


def solution(mesh):
    in_specs = (P("seq", None), P(), P("seq", "wt"), P("seq", None), P("wt", "seq"))
    return jax.shard_map(local, mesh=mesh, in_specs=in_specs, out_specs=P("seq", "wt"), check_vma=False)
```

```python
import math

import jax
import jax.numpy as jnp
import numpy as np
from jax import lax
from jax.experimental import pallas as pl
from jax.experimental.pallas import tpu as pltpu
from jax.sharding import PartitionSpec as P

MESH = pl.DeviceIdType.MESH
HEAD = 128
ROWS = 256
SHARDS = 16
BLOCK = 512
HEADS_HERE = 4
SCORE_LOG2 = math.log2(math.e) / math.sqrt(HEAD)
KV_WEIGHT, QUERY, OUTPUT, KEYS = 0, 1, 2, 3
f32 = jnp.float32
bf16 = jnp.bfloat16


def rope_constants():
    inverse = 500000.0 ** (-np.arange(HEAD // 2) * 2.0 / HEAD)
    wide = np.concatenate([inverse, inverse])
    sign = np.concatenate([-np.ones(HEAD // 2), np.ones(HEAD // 2)])
    inner = np.arange(ROWS)[:, None] * wide[None, :]
    outer = (np.arange(SHARDS) * ROWS)[:, None] * wide[None, :]
    outer = outer[:, None, :]
    return [np.stack([np.cos(t), np.sin(t) * sign]).astype(np.float32) for t in (inner, outer)]


def body(
    hidden_ref, gain_ref, wq_ref, wkv_ref, wo_ref, inner_ref, outer_ref, out_ref,
    inner, outer,
    hid, normed, wkv, wq, wo, kv, qacc, qrot, macc, oacc, heads, tacc, ysnd, yrcv,
    gsend, grecv, rsend, rrecv, dsend, drecv, xsend, xrecv, lsem,
):
    s = lax.axis_index("seq")
    w = lax.axis_index("wt")
    x, yl, core = lax.div(s, 4), lax.rem(lax.div(s, 2), 2), lax.rem(s, 2)
    yh, z = lax.div(w, 8), lax.rem(w, 8)
    xp, xm, xo = lax.rem(x + 1, 4), lax.rem(x + 3, 4), lax.rem(x + 2, 4)
    yp, sib_core = 1 - yl, 1 - core
    par = lax.rem(z, 2)
    chip = lax.div(s, 2)

    def sid(xi, yi, ci):
        return (xi * 2 + yi) * 2 + ci

    def wid(yi, zi):
        return yi * 8 + zi

    to_xp, to_xm = (sid(xp, yl, core), w), (sid(xm, yl, core), w)
    to_y, to_sib = (sid(x, yp, core), w), (sid(x, yl, sib_core), w)
    to_zp, to_zm = (s, wid(yh, lax.rem(z + 1, 8))), (s, wid(yh, lax.rem(z + 7, 8)))
    to_yh = (s, wid(1 - yh, z))
    to_pair = (s, wid(yh, z + 1 - 2 * par))

    barrier = pltpu.get_barrier_semaphore()
    for peer in (to_xp, to_xm, to_y, to_sib, to_zp, to_zm, to_yh):
        pl.semaphore_signal(barrier, inc=1, device_id=peer, device_id_type=MESH)
    keeps_piece = lax.rem(s, 8) == z
    deal_label = lax.div(s, 8) * 8 + z

    def greet(label):
        dealer = (z + 8 * lax.div(label, 8), wid(yh, lax.rem(label, 8)))
        pl.semaphore_signal(barrier, inc=1, device_id=dealer, device_id_type=MESH)

    for i in range(1, SHARDS):
        greet(lax.rem(deal_label + i, SHARDS))

    @pl.when(jnp.logical_not(keeps_piece))
    def _():
        greet(deal_label)

    first = pltpu.make_async_copy(
        wkv_ref.at[:, pl.ds(pl.multiple_of(w * HEAD, HEAD), HEAD)], wkv.at[s], lsem.at[0]
    )
    load_hidden = pltpu.make_async_copy(hidden_ref, hid, lsem.at[1])
    load_q = pltpu.make_async_copy(wq_ref, wq.at[s], lsem.at[2])
    load_inner = pltpu.make_async_copy(inner_ref, inner, lsem.at[4])
    load_outer = pltpu.make_async_copy(outer_ref.at[:, s], outer, lsem.at[5])
    first.start()
    load_hidden.start()
    load_q.start()
    load_inner.start()
    load_outer.start()
    pl.semaphore_wait(barrier, 7 + SHARDS - jnp.where(keeps_piece, 1, 0))

    stores = {KV_WEIGHT: wkv, QUERY: wq, OUTPUT: wo}

    def slot(k, shard, half=None):
        if k == KEYS:
            rows = pl.ds(pl.multiple_of(shard * ROWS, ROWS), ROWS)
            return kv.at[:, rows] if half is None else kv.at[half, rows]
        if half is None:
            return stores[k].at[shard]
        if k == OUTPUT:
            return wo.at[shard, half]
        return stores[k].at[shard, pl.ds(half * 256, 256)]

    started = []

    def send(k, label, source, place, peer):
        copy = pltpu.make_async_remote_copy(
            src_ref=source, dst_ref=place, send_sem=gsend.at[k, label], recv_sem=grecv.at[k, label],
            device_id=peer, device_id_type=MESH,
        )
        copy.start()
        started.append(copy)

    def forward(k, label, shard, peer, half=None):
        send(k, label, slot(k, shard, half), slot(k, shard, half), peer)

    def arrive(k, label, shard, half=None):
        place = slot(k, shard, half)
        pltpu.make_async_remote_copy(
            src_ref=place, dst_ref=place, send_sem=gsend.at[k, label], recv_sem=grecv.at[k, label],
            device_id=to_sib, device_id_type=MESH,
        ).wait_recv()

    chips = [(x, yl), (x, yp), (xm, yl), (xp, yl), (xm, yp), (xp, yp), (xo, yl), (xo, yp)]
    mine = [sid(a, b, core) for a, b in chips]
    theirs = [sid(a, b, sib_core) for a, b in chips]
    sib_label = [3, 9, 10, 11, 12, 13, 14, 15]

    def own_sends(k, source):
        for label, peer in ((0, to_xp), (1, to_xm), (2, to_y), (3, to_sib)):
            send(k, label, source, slot(k, s), peer)

    def near_x(k):
        arrive(k, 0, mine[2])
        forward(k, 6, mine[2], to_xp, 0)
        arrive(k, 1, mine[3])
        forward(k, 7, mine[3], to_xm, 1)
        for p in (2, 3):
            forward(k, sib_label[p], mine[p], to_sib)

    def near_y(k):
        arrive(k, 2, mine[1])
        forward(k, 4, mine[1], to_xp)
        forward(k, 5, mine[1], to_xm)
        forward(k, sib_label[1], mine[1], to_sib)

    def opposite(k):
        arrive(k, 6, mine[6], 0)
        arrive(k, 7, mine[6], 1)
        forward(k, 8, mine[6], to_y)
        forward(k, sib_label[6], mine[6], to_sib)

    def corners(k):
        for label, p in ((4, 4), (5, 5)):
            arrive(k, label, mine[p])
            forward(k, sib_label[p], mine[p], to_sib)

    def far(k):
        arrive(k, 8, mine[7])
        forward(k, sib_label[7], mine[7], to_sib)

    def from_sib(k, p):
        arrive(k, sib_label[p], theirs[p])

    first.wait()
    own_sends(KV_WEIGHT, wkv.at[s])

    def piece(p):
        return wo_ref.at[
            pl.ds(pl.multiple_of(lax.div(p, 4) * HEAD, HEAD), HEAD), pl.ds(pl.multiple_of(lax.rem(p, 4) * HEAD, HEAD), HEAD)
        ]

    def deal(i):
        p = lax.rem(s + i, SHARDS)
        return pltpu.make_async_remote_copy(
            src_ref=piece(p), dst_ref=wo.at[p, lax.div(s, 8), z], send_sem=dsend.at[i], recv_sem=drecv.at[deal_label],
            device_id=(p, wid(yh, lax.rem(s, 8))), device_id_type=MESH,
        )

    kept = pltpu.make_async_copy(piece(s), wo.at[s, lax.div(s, 8), z], lsem.at[3])
    def dealt(label):
        place = wo.at[s, lax.div(label, 8), lax.rem(label, 8)]
        pltpu.make_async_remote_copy(
            src_ref=place, dst_ref=place, send_sem=dsend.at[0], recv_sem=drecv.at[label], device_id=to_sib,
            device_id_type=MESH,
        ).wait_recv()

    def all_dealt():
        for i in range(1, SHARDS):
            dealt(lax.rem(deal_label + i, SHARDS))

        @pl.when(keeps_piece)
        def _():
            kept.wait()

        @pl.when(jnp.logical_not(keeps_piece))
        def _():
            dealt(deal_label)

    load_hidden.wait()

    def square(i, acc):
        block = hid[:, pl.ds(pl.multiple_of(i * BLOCK, BLOCK), BLOCK)].astype(f32)
        block = block * block
        return acc + (block[:, :128] + block[:, 128:256]) + (block[:, 256:384] + block[:, 384:])

    squares = lax.fori_loop(0, SHARDS, square, jnp.zeros((ROWS, 128), f32))
    inverse = lax.rsqrt(jnp.sum(squares, axis=1, keepdims=True) * (1.0 / 8192.0) + 1e-05)

    near_x(KV_WEIGHT)
    near_y(KV_WEIGHT)
    own_sends(QUERY, wq_ref)
    for i in range(1, SHARDS):
        deal(i).start()

    @pl.when(keeps_piece)
    def _():
        kept.start()

    @pl.when(jnp.logical_not(keeps_piece))
    def _():
        deal(0).start()


    def scale(i, _):
        columns = pl.ds(pl.multiple_of(i * BLOCK, BLOCK), BLOCK)
        block = hid[:, columns].astype(f32) * inverse * gain_ref[columns].astype(f32)
        normed[i] = block.astype(bf16)
        return 0

    lax.fori_loop(0, SHARDS, scale, 0)
    opposite(KV_WEIGHT)
    corners(KV_WEIGHT)
    far(KV_WEIGHT)

    for p in range(8):
        from_sib(KV_WEIGHT, p)

    def project(i, acc):
        return acc + jnp.dot(normed[i], wkv[i], preferred_element_type=f32)

    raw = lax.fori_loop(0, SHARDS, project, jnp.zeros((ROWS, HEAD), f32))
    load_inner.wait()
    load_outer.wait()
    cosines = outer[0] * inner[0] - outer[1] * inner[1]
    sines = outer[1] * inner[0] + outer[0] * inner[1]

    def rotate(u):
        return u * cosines + pltpu.roll(u, HEAD // 2, 1) * sines

    rows_here = pl.ds(pl.multiple_of(s * ROWS, ROWS), ROWS)
    is_value = (lax.broadcasted_iota(jnp.int32, (ROWS, HEAD), 0) * 0 + par) == 1
    kv[par, rows_here] = jnp.where(is_value, raw, rotate(raw)).astype(bf16)
    pair = pltpu.make_async_remote_copy(
        src_ref=kv.at[par, rows_here], dst_ref=kv.at[par, rows_here], send_sem=xsend.at[0], recv_sem=xrecv.at[0],
        device_id=to_pair, device_id_type=MESH,
    )
    pair.start()
    started.append(pair)
    load_q.wait()

    def accumulate(shard, start=False):
        term = jnp.dot(normed[shard], wq[shard], preferred_element_type=f32)
        qacc[...] = term if start else qacc[...] + term

    accumulate(mine[0], True)
    pltpu.make_async_remote_copy(
        src_ref=kv.at[1 - par, rows_here], dst_ref=kv.at[1 - par, rows_here], send_sem=xsend.at[0],
        recv_sem=xrecv.at[0], device_id=to_pair, device_id_type=MESH,
    ).wait_recv()
    own_sends(KEYS, slot(KEYS, s))
    near_x(QUERY)
    from_sib(QUERY, 0)
    accumulate(theirs[0])
    near_x(KEYS)
    near_y(KEYS)
    near_y(QUERY)
    all_dealt()
    own_sends(OUTPUT, wo.at[s])
    for p in (1, 2, 3):
        accumulate(mine[p])
    opposite(KEYS)
    corners(KEYS)
    opposite(QUERY)
    for p in (1, 2, 3):
        from_sib(QUERY, p)
        accumulate(theirs[p])
    far(KEYS)
    accumulate(mine[6])
    from_sib(QUERY, 6)
    accumulate(theirs[6])
    corners(QUERY)
    for p in (4, 5):
        accumulate(mine[p])
    far(QUERY)
    accumulate(mine[7])
    for p in (4, 5, 7):
        from_sib(QUERY, p)
        accumulate(theirs[p])
    for h in range(HEADS_HERE):
        qrot[h] = rotate(qacc[:, h * HEAD : (h + 1) * HEAD]).astype(bf16)
    for p in range(8):
        from_sib(KEYS, p)

    ones = jnp.ones((BLOCK, HEAD), bf16)

    def scores_of(h, block):
        rows = pl.ds(pl.multiple_of(block * BLOCK, BLOCK), BLOCK)
        return lax.dot_general(
            qrot[h], kv[0, rows], (((1,), (1,)), ((), ())), preferred_element_type=f32
        )

    def values_of(block):
        rows = pl.ds(pl.multiple_of(block * BLOCK, BLOCK), BLOCK)
        return jnp.concatenate([kv[1, rows], ones], axis=1)

    query_at = lax.broadcasted_iota(jnp.int32, (ROWS, BLOCK), 0) + core * ROWS
    allowed = lax.broadcasted_iota(jnp.int32, (ROWS, BLOCK), 1) <= query_at
    def hop(label, source, place, peer):
        copy = pltpu.make_async_remote_copy(
            src_ref=source, dst_ref=place, send_sem=rsend.at[label], recv_sem=rrecv.at[label],
            device_id=peer, device_id_type=MESH,
        )
        copy.start()
        started.append(copy)

    def landed(label, place):
        pltpu.make_async_remote_copy(
            src_ref=place, dst_ref=place, send_sem=rsend.at[label], recv_sem=rrecv.at[label],
            device_id=to_sib, device_id_type=MESH,
        ).wait_recv()

    def zplace(source, h, half=None):
        return heads.at[source, h] if half is None else heads.at[source, h, pl.ds(half * 128, 128)]

    def zsource(way, d):
        return lax.rem(z + 8 - d, 8) if way == 0 else lax.rem(z + d, 8)

    def zsend(h, way, d):
        place = zplace(zsource(way, d - 1), h, way if d == 4 else None)
        hop((h * 2 + way) * 4 + d - 1, place, place, (to_zp, to_zm)[way])

    def zland(h, way, d):
        landed((h * 2 + way) * 4 + d - 1, zplace(zsource(way, d), h, way if d == 4 else None))

    def wave(turn):
        for d in (1, 2, 3, 4):
            h = turn - d
            if 0 <= h < HEADS_HERE:
                for way in range(2):
                    zland(h, way, d)
                    if d < 4:
                        zsend(h, way, d + 1)

    for pair_first in (0, 2):
        both = (pair_first, pair_first + 1)
        for h in both:
            scores = jnp.where(allowed, scores_of(h, chip), -1e30)
            high = jnp.max(scores, axis=1, keepdims=True)
            weights = jnp.exp2((scores - high) * SCORE_LOG2).astype(bf16)
            oacc[h] = jnp.dot(weights, values_of(chip), preferred_element_type=f32)
            macc[h] = jnp.broadcast_to(high, (ROWS, HEAD))

        def attend(block, _, both=both):
            values = values_of(block)
            for h in both:
                scores = scores_of(h, block)
                before = macc[h][:, :1]
                high = jnp.maximum(before, jnp.max(scores, axis=1, keepdims=True))
                weights = jnp.exp2((scores - high) * SCORE_LOG2).astype(bf16)
                keep = jnp.exp2((before - high) * SCORE_LOG2)
                oacc[h] = oacc[h] * keep + jnp.dot(weights, values, preferred_element_type=f32)
                macc[h] = jnp.broadcast_to(high, (ROWS, HEAD))
            return 0

        lax.fori_loop(0, chip, attend, 0)
        for h in both:
            heads[z, h] = (oacc[h][:, :HEAD] / oacc[h][:, HEAD:]).astype(bf16)
            zsend(h, 0, 1)
            zsend(h, 1, 1)
        if pair_first == 0:
            near_x(OUTPUT)
            near_y(OUTPUT)
            wave(1)
    wave(2)
    wave(3)
    opposite(OUTPUT)
    for turn in range(HEADS_HERE, HEADS_HERE + 4):
        wave(turn)
    corners(OUTPUT)
    far(OUTPUT)

    def columns_from(p, fresh):
        row, column = chips[p]
        place = row * 2 + column
        left = jnp.concatenate([heads[i, row] for i in range(8)], axis=1)
        for yi in range(2):
            right = jnp.concatenate(
                [wo[place * 2 + i, yi].reshape(8 * HEAD, HEAD) for i in range(2)], axis=1
            )
            term = jnp.dot(left, right, preferred_element_type=f32)
            tacc[yi, column] = term if fresh else tacc[yi, column] + term

    for n, (column, positions) in enumerate(((yl, (0, 2, 3, 6)), (yp, (1, 4, 5, 7)))):
        for p in positions:
            from_sib(OUTPUT, p)
            columns_from(p, p < 2)
        ysnd[column] = tacc[1 - yh, column].astype(bf16)
        hop(32 + n, ysnd.at[column], yrcv.at[column], to_yh)
    for n, column in enumerate((yl, yp)):
        landed(32 + n, yrcv.at[column])
        at = pl.ds(pl.multiple_of(column * 256, 256), 256)
        wide = pl.ds(pl.multiple_of(w * BLOCK + column * 256, 256), 256)
        out_ref[:, at] = (hid[:, wide].astype(f32) + tacc[yh, column] + yrcv[column].astype(f32)).astype(bf16)
    for copy in started:
        copy.wait_send()
    for i in range(1, SHARDS):
        deal(i).wait_send()

    @pl.when(jnp.logical_not(keeps_piece))
    def _():
        deal(0).wait_send()


def local(hidden_states, norm_gain, query_weight, key_value_matrix, output_weight):
    tables = [jnp.asarray(t) for t in rope_constants()]
    anywhere = pl.BlockSpec(memory_space=pl.ANY)
    inside = pl.BlockSpec(memory_space=pltpu.VMEM)
    dma = pltpu.SemaphoreType.DMA
    return pl.pallas_call(
        body,
        out_shape=jax.ShapeDtypeStruct((ROWS, BLOCK), bf16),
        in_specs=[anywhere, inside, anywhere, anywhere, anywhere] + [anywhere] * 2,
        out_specs=inside,
        scratch_shapes=[
            pltpu.VMEM((2, ROWS, HEAD), f32),
            pltpu.VMEM((2, 1, HEAD), f32),
            pltpu.VMEM((ROWS, 8192), bf16),
            pltpu.VMEM((SHARDS, ROWS, BLOCK), bf16),
            pltpu.VMEM((SHARDS, BLOCK, HEAD), bf16),
            pltpu.VMEM((SHARDS, BLOCK, BLOCK), bf16),
            pltpu.VMEM((SHARDS, 2, 8, HEAD, HEAD), bf16),
            pltpu.VMEM((2, SHARDS * ROWS, HEAD), bf16),
            pltpu.VMEM((ROWS, BLOCK), f32),
            pltpu.VMEM((HEADS_HERE, ROWS, HEAD), bf16),
            pltpu.VMEM((HEADS_HERE, ROWS, HEAD), f32),
            pltpu.VMEM((HEADS_HERE, ROWS, 2 * HEAD), f32),
            pltpu.VMEM((8, HEADS_HERE, ROWS, HEAD), bf16),
            pltpu.VMEM((2, 2, ROWS, 256), f32),
            pltpu.VMEM((2, ROWS, 256), bf16),
            pltpu.VMEM((2, ROWS, 256), bf16),
            dma((4, 16)),
            dma((4, 16)),
            dma((34,)),
            dma((34,)),
            dma((16,)),
            dma((16,)),
            dma((1,)),
            dma((1,)),
            dma((6,)),
        ],
        compiler_params=pltpu.CompilerParams(
            collective_id=0, has_side_effects=True, vmem_limit_bytes=56 * 1024 * 1024
        ),
    )(hidden_states, norm_gain, query_weight, key_value_matrix, output_weight, *tables)


def solution(mesh):
    in_specs = (P("seq", None), P(), P("seq", "wt"), P("seq", None), P("wt", "seq"))
    return jax.shard_map(local, mesh=mesh, in_specs=in_specs, out_specs=P("seq", "wt"), check_vma=False)
```

```python
import math

import jax
import jax.numpy as jnp
import numpy as np
from jax import lax
from jax.experimental import pallas as pl
from jax.experimental.pallas import tpu as pltpu
from jax.sharding import PartitionSpec as P

MESH = pl.DeviceIdType.MESH
HEAD = 128
ROWS = 256
SHARDS = 16
BLOCK = 512
HEADS_HERE = 4
SCORE_LOG2 = math.log2(math.e) / math.sqrt(HEAD)
KV_WEIGHT, QUERY, OUTPUT, KEYS = 0, 1, 2, 3
f32 = jnp.float32
bf16 = jnp.bfloat16


def rope_constants():
    inverse = 500000.0 ** (-np.arange(HEAD // 2) * 2.0 / HEAD)
    wide = np.concatenate([inverse, inverse])
    sign = np.concatenate([-np.ones(HEAD // 2), np.ones(HEAD // 2)])
    inner = np.arange(ROWS)[:, None] * wide[None, :]
    outer = (np.arange(SHARDS) * ROWS)[:, None] * wide[None, :]
    outer = outer[:, None, :]
    return [np.stack([np.cos(t), np.sin(t) * sign]).astype(np.float32) for t in (inner, outer)]


def body(
    hidden_ref, gain_ref, wq_ref, wkv_ref, wo_ref, inner_ref, outer_ref, out_ref,
    inner, outer,
    hid, normed, wkv, wq, wo, pieces, kv, qacc, qrot, macc, oacc, heads, tacc, ysnd, yrcv,
    gsend, grecv, rsend, rrecv, dsend, drecv, xsend, xrecv, lsem,
):
    s = lax.axis_index("seq")
    w = lax.axis_index("wt")
    x, yl, core = lax.div(s, 4), lax.rem(lax.div(s, 2), 2), lax.rem(s, 2)
    yh, z = lax.div(w, 8), lax.rem(w, 8)
    xp, xm, xo = lax.rem(x + 1, 4), lax.rem(x + 3, 4), lax.rem(x + 2, 4)
    yp, sib_core = 1 - yl, 1 - core
    par = lax.rem(z, 2)
    chip = lax.div(s, 2)

    def sid(xi, yi, ci):
        return (xi * 2 + yi) * 2 + ci

    def wid(yi, zi):
        return yi * 8 + zi

    to_xp, to_xm = (sid(xp, yl, core), w), (sid(xm, yl, core), w)
    to_y, to_sib = (sid(x, yp, core), w), (sid(x, yl, sib_core), w)
    to_zp, to_zm = (s, wid(yh, lax.rem(z + 1, 8))), (s, wid(yh, lax.rem(z + 7, 8)))
    to_yh = (s, wid(1 - yh, z))
    to_pair = (s, wid(yh, z + 1 - 2 * par))

    barrier = pltpu.get_barrier_semaphore()
    for peer in (to_xp, to_xm, to_y, to_sib, to_zp, to_zm, to_yh):
        pl.semaphore_signal(barrier, inc=1, device_id=peer, device_id_type=MESH)
    plane = [(sid(xi, yi, ci), w) for xi in (x, xp, xm, xo) for yi in (yl, yp) for ci in (core, sib_core)]
    ring = [lax.rem(z + d, 8) for d in range(8)]
    others = [peer for n, peer in enumerate(plane) if n not in (0, 1, 2, 4, 8)]
    others += [(s, wid(yh, ring[d])) for d in range(2, 7)]
    for peer in others:
        pl.semaphore_signal(barrier, inc=1, device_id=peer, device_id_type=MESH)

    first = pltpu.make_async_copy(
        wkv_ref.at[:, pl.ds(pl.multiple_of(w * HEAD, HEAD), HEAD)], wkv.at[s], lsem.at[0]
    )
    load_hidden = pltpu.make_async_copy(hidden_ref, hid, lsem.at[1])
    load_q = pltpu.make_async_copy(wq_ref, wq.at[s], lsem.at[2])
    load_inner = pltpu.make_async_copy(inner_ref, inner, lsem.at[4])
    load_outer = pltpu.make_async_copy(outer_ref.at[:, s], outer, lsem.at[5])
    first.start()
    load_hidden.start()
    load_q.start()
    load_inner.start()
    load_outer.start()
    pl.semaphore_wait(barrier, 7 + len(others))

    stores = {KV_WEIGHT: wkv, QUERY: wq, OUTPUT: wo}

    def slot(k, shard, half=None):
        if k == KEYS:
            rows = pl.ds(pl.multiple_of(shard * ROWS, ROWS), ROWS)
            return kv.at[:, rows] if half is None else kv.at[half, rows]
        if half is None:
            return stores[k].at[shard]
        if k == OUTPUT:
            return wo.at[shard, half]
        return stores[k].at[shard, pl.ds(half * 256, 256)]

    started = []

    def send(k, label, source, place, peer):
        copy = pltpu.make_async_remote_copy(
            src_ref=source, dst_ref=place, send_sem=gsend.at[k, label], recv_sem=grecv.at[k, label],
            device_id=peer, device_id_type=MESH,
        )
        copy.start()
        started.append(copy)

    def forward(k, label, shard, peer, half=None):
        send(k, label, slot(k, shard, half), slot(k, shard, half), peer)

    def arrive(k, label, shard, half=None):
        place = slot(k, shard, half)
        pltpu.make_async_remote_copy(
            src_ref=place, dst_ref=place, send_sem=gsend.at[k, label], recv_sem=grecv.at[k, label],
            device_id=to_sib, device_id_type=MESH,
        ).wait_recv()

    chips = [(x, yl), (x, yp), (xm, yl), (xp, yl), (xm, yp), (xp, yp), (xo, yl), (xo, yp)]
    mine = [sid(a, b, core) for a, b in chips]
    theirs = [sid(a, b, sib_core) for a, b in chips]
    sib_label = [3, 9, 10, 11, 12, 13, 14, 15]

    def own_x(k, source):
        for label, peer in ((0, to_xp), (1, to_xm), (3, to_sib)):
            send(k, label, source, slot(k, s), peer)

    def own_y(k, source):
        send(k, 2, source, slot(k, s), to_y)

    def own_sends(k, source):
        own_x(k, source)
        own_y(k, source)

    def near_x(k):
        arrive(k, 0, mine[2])
        forward(k, 6, mine[2], to_xp, 0)
        arrive(k, 1, mine[3])
        forward(k, 7, mine[3], to_xm, 1)
        for p in (2, 3):
            forward(k, sib_label[p], mine[p], to_sib)

    def near_y(k):
        arrive(k, 2, mine[1])
        forward(k, 4, mine[1], to_xp)
        forward(k, 5, mine[1], to_xm)
        forward(k, sib_label[1], mine[1], to_sib)

    def opposite(k):
        arrive(k, 6, mine[6], 0)
        arrive(k, 7, mine[6], 1)
        forward(k, 8, mine[6], to_y)
        forward(k, sib_label[6], mine[6], to_sib)

    def corners(k):
        for label, p in ((4, 4), (5, 5)):
            arrive(k, label, mine[p])
            forward(k, sib_label[p], mine[p], to_sib)

    def far(k):
        arrive(k, 8, mine[7])
        forward(k, sib_label[7], mine[7], to_sib)

    def from_sib(k, p):
        arrive(k, sib_label[p], theirs[p])

    first.wait()
    own_sends(KV_WEIGHT, wkv.at[s])

    def piece(p):
        return wo_ref.at[
            pl.ds(pl.multiple_of(lax.div(p, 4) * HEAD, HEAD), HEAD), pl.ds(pl.multiple_of(lax.rem(p, 4) * HEAD, HEAD), HEAD)
        ]

    def part(label, source, place, peer):
        copy = pltpu.make_async_remote_copy(
            src_ref=source, dst_ref=place, send_sem=dsend.at[label], recv_sem=drecv.at[label],
            device_id=peer, device_id_type=MESH,
        )
        return copy

    keep_piece = pltpu.make_async_copy(piece(s), pieces.at[lax.div(s, 8), lax.rem(s, 8)], lsem.at[3])
    keep_rows = pltpu.make_async_copy(pieces.at[:, z], wo.at[s, :, z], lsem.at[2])

    def spread():
        keep_piece.start()
        for n in range(1, SHARDS):
            copy = part(n, piece(plane[n][0]), pieces.at[lax.div(s, 8), lax.rem(s, 8)], plane[n])
            copy.start()
            started.append(copy)

    senders = [(sid(xi, yi, ci), w) for xi in (x, xm, xp, xo) for yi in (yl, yp) for ci in (core, sib_core)]

    def deal():
        keep_piece.wait()
        for n in range(1, SHARDS):
            place = pieces.at[lax.div(senders[n][0], 8), lax.rem(senders[n][0], 8)]
            part(n, place, place, to_sib).wait_recv()
        keep_rows.start()
        for d in (4, 3, 5, 2, 6, 1, 7):
            copy = part(15 + d, pieces.at[:, ring[d]], wo.at[s, :, z], (s, wid(yh, ring[d])))
            copy.start()
            started.append(copy)

    def all_dealt():
        keep_rows.wait()
        for d in range(1, 8):
            place = wo.at[s, :, ring[8 - d]]
            part(15 + d, place, place, to_sib).wait_recv()

    load_hidden.wait()

    def square(i, acc):
        block = hid[:, pl.ds(pl.multiple_of(i * BLOCK, BLOCK), BLOCK)].astype(f32)
        block = block * block
        return acc + (block[:, :128] + block[:, 128:256]) + (block[:, 256:384] + block[:, 384:])

    squares = lax.fori_loop(0, SHARDS, square, jnp.zeros((ROWS, 128), f32))
    inverse = lax.rsqrt(jnp.sum(squares, axis=1, keepdims=True) * (1.0 / 8192.0) + 1e-05)

    near_x(KV_WEIGHT)
    near_y(KV_WEIGHT)
    own_x(QUERY, wq_ref)
    opposite(KV_WEIGHT)
    own_y(QUERY, wq_ref)


    def scale(i, _):
        columns = pl.ds(pl.multiple_of(i * BLOCK, BLOCK), BLOCK)
        block = hid[:, columns].astype(f32) * inverse * gain_ref[columns].astype(f32)
        normed[i] = block.astype(bf16)
        return 0

    lax.fori_loop(0, SHARDS, scale, 0)
    corners(KV_WEIGHT)
    far(KV_WEIGHT)

    for p in range(8):
        from_sib(KV_WEIGHT, p)

    def project(i, acc):
        return acc + jnp.dot(normed[i], wkv[i], preferred_element_type=f32)

    raw = lax.fori_loop(0, SHARDS, project, jnp.zeros((ROWS, HEAD), f32))
    load_inner.wait()
    load_outer.wait()
    cosines = outer[0] * inner[0] - outer[1] * inner[1]
    sines = outer[1] * inner[0] + outer[0] * inner[1]

    def rotate(u):
        return u * cosines + pltpu.roll(u, HEAD // 2, 1) * sines

    rows_here = pl.ds(pl.multiple_of(s * ROWS, ROWS), ROWS)
    is_value = (lax.broadcasted_iota(jnp.int32, (ROWS, HEAD), 0) * 0 + par) == 1
    kv[par, rows_here] = jnp.where(is_value, raw, rotate(raw)).astype(bf16)
    pair = pltpu.make_async_remote_copy(
        src_ref=kv.at[par, rows_here], dst_ref=kv.at[par, rows_here], send_sem=xsend.at[0], recv_sem=xrecv.at[0],
        device_id=to_pair, device_id_type=MESH,
    )
    pair.start()
    started.append(pair)
    load_q.wait()

    def accumulate(shard, start=False):
        term = jnp.dot(normed[shard], wq[shard], preferred_element_type=f32)
        qacc[...] = term if start else qacc[...] + term

    accumulate(mine[0], True)
    pltpu.make_async_remote_copy(
        src_ref=kv.at[1 - par, rows_here], dst_ref=kv.at[1 - par, rows_here], send_sem=xsend.at[0],
        recv_sem=xrecv.at[0], device_id=to_pair, device_id_type=MESH,
    ).wait_recv()
    own_sends(KEYS, slot(KEYS, s))
    spread()
    near_x(QUERY)
    from_sib(QUERY, 0)
    accumulate(theirs[0])
    near_x(KEYS)
    near_y(KEYS)
    near_y(QUERY)
    accumulate(mine[1])
    accumulate(mine[2])
    deal()
    accumulate(mine[3])
    for p in (1, 2, 3):
        from_sib(QUERY, p)
        accumulate(theirs[p])
    opposite(QUERY)
    opposite(KEYS)
    corners(KEYS)
    far(KEYS)
    all_dealt()
    own_sends(OUTPUT, wo.at[s])
    accumulate(mine[6])
    from_sib(QUERY, 6)
    accumulate(theirs[6])
    corners(QUERY)
    for p in (4, 5):
        accumulate(mine[p])
    far(QUERY)
    accumulate(mine[7])
    for p in (4, 5, 7):
        from_sib(QUERY, p)
        accumulate(theirs[p])
    for h in range(HEADS_HERE):
        qrot[h] = rotate(qacc[:, h * HEAD : (h + 1) * HEAD]).astype(bf16)
    for p in range(8):
        from_sib(KEYS, p)

    ones = jnp.ones((BLOCK, HEAD), bf16)

    def scores_of(h, block):
        rows = pl.ds(pl.multiple_of(block * BLOCK, BLOCK), BLOCK)
        return lax.dot_general(
            qrot[h], kv[0, rows], (((1,), (1,)), ((), ())), preferred_element_type=f32
        )

    def values_of(block):
        rows = pl.ds(pl.multiple_of(block * BLOCK, BLOCK), BLOCK)
        return jnp.concatenate([kv[1, rows], ones], axis=1)

    query_at = lax.broadcasted_iota(jnp.int32, (ROWS, BLOCK), 0) + core * ROWS
    allowed = lax.broadcasted_iota(jnp.int32, (ROWS, BLOCK), 1) <= query_at
    def hop(label, source, place, peer):
        copy = pltpu.make_async_remote_copy(
            src_ref=source, dst_ref=place, send_sem=rsend.at[label], recv_sem=rrecv.at[label],
            device_id=peer, device_id_type=MESH,
        )
        copy.start()
        started.append(copy)

    def landed(label, place):
        pltpu.make_async_remote_copy(
            src_ref=place, dst_ref=place, send_sem=rsend.at[label], recv_sem=rrecv.at[label],
            device_id=to_sib, device_id_type=MESH,
        ).wait_recv()

    def zplace(source, h, half=None):
        return heads.at[source, h] if half is None else heads.at[source, h, pl.ds(half * 128, 128)]

    def zsource(way, d):
        return lax.rem(z + 8 - d, 8) if way == 0 else lax.rem(z + d, 8)

    def zsend(h, way, d):
        place = zplace(zsource(way, d - 1), h, way if d == 4 else None)
        hop((h * 2 + way) * 4 + d - 1, place, place, (to_zp, to_zm)[way])

    def zland(h, way, d):
        landed((h * 2 + way) * 4 + d - 1, zplace(zsource(way, d), h, way if d == 4 else None))

    def zstep(first, d):
        for h in (first, first + 1):
            for way in range(2):
                zland(h, way, d)
                if d < 4:
                    zsend(h, way, d + 1)

    for pair_first in (0, 2):
        both = (pair_first, pair_first + 1)
        for h in both:
            scores = jnp.where(allowed, scores_of(h, chip), -1e30)
            high = jnp.max(scores, axis=1, keepdims=True)
            weights = jnp.exp2((scores - high) * SCORE_LOG2).astype(bf16)
            oacc[h] = jnp.dot(weights, values_of(chip), preferred_element_type=f32)
            macc[h] = jnp.broadcast_to(high, (ROWS, HEAD))

        def attend(block, _, both=both):
            values = values_of(block)
            for h in both:
                scores = scores_of(h, block)
                before = macc[h][:, :1]
                high = jnp.maximum(before, jnp.max(scores, axis=1, keepdims=True))
                weights = jnp.exp2((scores - high) * SCORE_LOG2).astype(bf16)
                keep = jnp.exp2((before - high) * SCORE_LOG2)
                oacc[h] = oacc[h] * keep + jnp.dot(weights, values, preferred_element_type=f32)
                macc[h] = jnp.broadcast_to(high, (ROWS, HEAD))
            return 0

        lax.fori_loop(0, jnp.minimum(chip, 4), attend, 0)
        if pair_first == 2:
            zstep(0, 1)
            near_x(OUTPUT)
            near_y(OUTPUT)
        lax.fori_loop(4, jnp.maximum(chip, 4), attend, 0)
        for h in both:
            heads[z, h] = (oacc[h][:, :HEAD] / oacc[h][:, HEAD:]).astype(bf16)
            zsend(h, 0, 1)
            zsend(h, 1, 1)
    zstep(0, 2)
    zstep(2, 1)
    opposite(OUTPUT)
    zstep(0, 3)
    zstep(2, 2)
    zstep(0, 4)
    zstep(2, 3)
    zstep(2, 4)
    corners(OUTPUT)
    far(OUTPUT)

    def columns_from(p, fresh):
        row, column = chips[p]
        place = row * 2 + column
        left = jnp.concatenate([heads[i, row] for i in range(8)], axis=1)
        for yi in range(2):
            right = jnp.concatenate(
                [wo[place * 2 + i, yi].reshape(8 * HEAD, HEAD) for i in range(2)], axis=1
            )
            term = jnp.dot(left, right, preferred_element_type=f32)
            tacc[yi, column] = term if fresh else tacc[yi, column] + term

    for n, (column, positions) in enumerate(((yl, (0, 2, 3, 6)), (yp, (1, 4, 5, 7)))):
        for p in positions:
            from_sib(OUTPUT, p)
            columns_from(p, p < 2)
        ysnd[column] = tacc[1 - yh, column].astype(bf16)
        hop(32 + n, ysnd.at[column], yrcv.at[column], to_yh)
    for n, column in enumerate((yl, yp)):
        landed(32 + n, yrcv.at[column])
        at = pl.ds(pl.multiple_of(column * 256, 256), 256)
        wide = pl.ds(pl.multiple_of(w * BLOCK + column * 256, 256), 256)
        out_ref[:, at] = (hid[:, wide].astype(f32) + tacc[yh, column] + yrcv[column].astype(f32)).astype(bf16)
    for copy in started:
        copy.wait_send()


def local(hidden_states, norm_gain, query_weight, key_value_matrix, output_weight):
    tables = [jnp.asarray(t) for t in rope_constants()]
    anywhere = pl.BlockSpec(memory_space=pl.ANY)
    inside = pl.BlockSpec(memory_space=pltpu.VMEM)
    dma = pltpu.SemaphoreType.DMA
    return pl.pallas_call(
        body,
        out_shape=jax.ShapeDtypeStruct((ROWS, BLOCK), bf16),
        in_specs=[anywhere, inside, anywhere, anywhere, anywhere] + [anywhere] * 2,
        out_specs=inside,
        scratch_shapes=[
            pltpu.VMEM((2, ROWS, HEAD), f32),
            pltpu.VMEM((2, 1, HEAD), f32),
            pltpu.VMEM((ROWS, 8192), bf16),
            pltpu.VMEM((SHARDS, ROWS, BLOCK), bf16),
            pltpu.VMEM((SHARDS, BLOCK, HEAD), bf16),
            pltpu.VMEM((SHARDS, BLOCK, BLOCK), bf16),
            pltpu.VMEM((SHARDS, 2, 8, HEAD, HEAD), bf16),
            pltpu.VMEM((2, 8, HEAD, HEAD), bf16),
            pltpu.VMEM((2, SHARDS * ROWS, HEAD), bf16),
            pltpu.VMEM((ROWS, BLOCK), f32),
            pltpu.VMEM((HEADS_HERE, ROWS, HEAD), bf16),
            pltpu.VMEM((HEADS_HERE, ROWS, HEAD), f32),
            pltpu.VMEM((HEADS_HERE, ROWS, 2 * HEAD), f32),
            pltpu.VMEM((8, HEADS_HERE, ROWS, HEAD), bf16),
            pltpu.VMEM((2, 2, ROWS, 256), f32),
            pltpu.VMEM((2, ROWS, 256), bf16),
            pltpu.VMEM((2, ROWS, 256), bf16),
            dma((4, 16)),
            dma((4, 16)),
            dma((34,)),
            dma((34,)),
            dma((23,)),
            dma((23,)),
            dma((1,)),
            dma((1,)),
            dma((6,)),
        ],
        compiler_params=pltpu.CompilerParams(
            collective_id=0, has_side_effects=True, vmem_limit_bytes=56 * 1024 * 1024
        ),
    )(hidden_states, norm_gain, query_weight, key_value_matrix, output_weight, *tables)


def solution(mesh):
    in_specs = (P("seq", None), P(), P("seq", "wt"), P("seq", None), P("wt", "seq"))
    return jax.shard_map(local, mesh=mesh, in_specs=in_specs, out_specs=P("seq", "wt"), check_vma=False)
```

```python
import math

import jax
import jax.numpy as jnp
import numpy as np
from jax import lax
from jax.experimental import pallas as pl
from jax.experimental.pallas import tpu as pltpu
from jax.sharding import PartitionSpec as P

MESH = pl.DeviceIdType.MESH
HEAD = 128
ROWS = 256
SHARDS = 16
BLOCK = 512
HEADS_HERE = 4
SCORE_LOG2 = math.log2(math.e) / math.sqrt(HEAD)
KV_WEIGHT, QUERY, OUTPUT, KEYS = 0, 1, 2, 3
f32 = jnp.float32
bf16 = jnp.bfloat16


def rope_constants():
    inverse = 500000.0 ** (-np.arange(HEAD // 2) * 2.0 / HEAD)
    wide = np.concatenate([inverse, inverse])
    sign = np.concatenate([-np.ones(HEAD // 2), np.ones(HEAD // 2)])
    inner = np.arange(ROWS)[:, None] * wide[None, :]
    outer = (np.arange(SHARDS) * ROWS)[:, None] * wide[None, :]
    outer = outer[:, None, :]
    return [np.stack([np.cos(t), np.sin(t) * sign]).astype(np.float32) for t in (inner, outer)]


def body(
    hidden_ref, gain_ref, wq_ref, wkv_ref, wo_ref, inner_ref, outer_ref, out_ref,
    inner, outer,
    hid, normed, wkv, wq, wo, pieces, kv, qacc, qrot, macc, oacc, heads, tacc, ysnd, yrcv,
    gsend, grecv, rsend, rrecv, dsend, drecv, xsend, xrecv, lsem,
):
    s = lax.axis_index("seq")
    w = lax.axis_index("wt")
    x, yl, core = lax.div(s, 4), lax.rem(lax.div(s, 2), 2), lax.rem(s, 2)
    yh, z = lax.div(w, 8), lax.rem(w, 8)
    xp, xm, xo = lax.rem(x + 1, 4), lax.rem(x + 3, 4), lax.rem(x + 2, 4)
    yp, sib_core = 1 - yl, 1 - core
    par = lax.rem(z, 2)
    chip = lax.div(s, 2)

    def sid(xi, yi, ci):
        return (xi * 2 + yi) * 2 + ci

    def wid(yi, zi):
        return yi * 8 + zi

    to_xp, to_xm = (sid(xp, yl, core), w), (sid(xm, yl, core), w)
    to_y, to_sib = (sid(x, yp, core), w), (sid(x, yl, sib_core), w)
    to_zp, to_zm = (s, wid(yh, lax.rem(z + 1, 8))), (s, wid(yh, lax.rem(z + 7, 8)))
    to_yh = (s, wid(1 - yh, z))
    to_pair = (s, wid(yh, z + 1 - 2 * par))

    barrier = pltpu.get_barrier_semaphore()
    for peer in (to_xp, to_xm, to_y, to_sib, to_zp, to_zm, to_yh):
        pl.semaphore_signal(barrier, inc=1, device_id=peer, device_id_type=MESH)
    plane = [(sid(xi, yi, ci), w) for xi in (x, xp, xm, xo) for yi in (yl, yp) for ci in (core, sib_core)]
    ring = [lax.rem(z + d, 8) for d in range(8)]
    others = [peer for n, peer in enumerate(plane) if n not in (0, 1, 2, 4, 8)]
    others += [(s, wid(yh, ring[d])) for d in range(2, 7)]
    for peer in others:
        pl.semaphore_signal(barrier, inc=1, device_id=peer, device_id_type=MESH)

    first = pltpu.make_async_copy(
        wkv_ref.at[:, pl.ds(pl.multiple_of(w * HEAD, HEAD), HEAD)], wkv.at[s], lsem.at[0]
    )
    load_hidden = pltpu.make_async_copy(hidden_ref, hid, lsem.at[1])
    load_q = pltpu.make_async_copy(wq_ref, wq.at[s], lsem.at[2])
    load_inner = pltpu.make_async_copy(inner_ref, inner, lsem.at[4])
    load_outer = pltpu.make_async_copy(outer_ref.at[:, s], outer, lsem.at[5])
    first.start()
    load_hidden.start()
    load_q.start()
    load_inner.start()
    load_outer.start()
    pl.semaphore_wait(barrier, 7 + len(others))

    stores = {KV_WEIGHT: wkv, QUERY: wq, OUTPUT: wo}

    def slot(k, shard, half=None):
        if k == KEYS:
            rows = pl.ds(pl.multiple_of(shard * ROWS, ROWS), ROWS)
            return kv.at[:, rows] if half is None else kv.at[half, rows]
        if half is None:
            return stores[k].at[shard]
        if k == OUTPUT:
            return wo.at[shard, half]
        return stores[k].at[shard, pl.ds(half * 256, 256)]

    started = []

    def send(k, label, source, place, peer):
        copy = pltpu.make_async_remote_copy(
            src_ref=source, dst_ref=place, send_sem=gsend.at[k, label], recv_sem=grecv.at[k, label],
            device_id=peer, device_id_type=MESH,
        )
        copy.start()
        started.append(copy)

    def forward(k, label, shard, peer, half=None):
        send(k, label, slot(k, shard, half), slot(k, shard, half), peer)

    def arrive(k, label, shard, half=None):
        place = slot(k, shard, half)
        pltpu.make_async_remote_copy(
            src_ref=place, dst_ref=place, send_sem=gsend.at[k, label], recv_sem=grecv.at[k, label],
            device_id=to_sib, device_id_type=MESH,
        ).wait_recv()

    chips = [(x, yl), (x, yp), (xm, yl), (xp, yl), (xm, yp), (xp, yp), (xo, yl), (xo, yp)]
    mine = [sid(a, b, core) for a, b in chips]
    theirs = [sid(a, b, sib_core) for a, b in chips]
    sib_label = [3, 9, 10, 11, 12, 13, 14, 15]

    def own_x(k, source):
        for label, peer in ((0, to_xp), (1, to_xm), (3, to_sib)):
            send(k, label, source, slot(k, s), peer)

    def own_y(k, source):
        send(k, 2, source, slot(k, s), to_y)

    def own_sends(k, source):
        own_x(k, source)
        own_y(k, source)

    def near_x(k):
        arrive(k, 0, mine[2])
        forward(k, 6, mine[2], to_xp, 0)
        arrive(k, 1, mine[3])
        forward(k, 7, mine[3], to_xm, 1)
        for p in (2, 3):
            forward(k, sib_label[p], mine[p], to_sib)

    def near_y(k):
        arrive(k, 2, mine[1])
        forward(k, 4, mine[1], to_xp)
        forward(k, 5, mine[1], to_xm)
        forward(k, sib_label[1], mine[1], to_sib)

    def opposite(k):
        arrive(k, 6, mine[6], 0)
        arrive(k, 7, mine[6], 1)
        forward(k, 8, mine[6], to_y)
        forward(k, sib_label[6], mine[6], to_sib)

    def corners(k):
        for label, p in ((4, 4), (5, 5)):
            arrive(k, label, mine[p])
            forward(k, sib_label[p], mine[p], to_sib)

    def far(k):
        arrive(k, 8, mine[7])
        forward(k, sib_label[7], mine[7], to_sib)

    def from_sib(k, p):
        arrive(k, sib_label[p], theirs[p])

    first.wait()
    own_sends(KV_WEIGHT, wkv.at[s])

    def piece(p):
        return wo_ref.at[
            pl.ds(pl.multiple_of(lax.div(p, 4) * HEAD, HEAD), HEAD), pl.ds(pl.multiple_of(lax.rem(p, 4) * HEAD, HEAD), HEAD)
        ]

    def part(label, source, place, peer):
        copy = pltpu.make_async_remote_copy(
            src_ref=source, dst_ref=place, send_sem=dsend.at[label], recv_sem=drecv.at[label],
            device_id=peer, device_id_type=MESH,
        )
        return copy

    keep_piece = pltpu.make_async_copy(piece(s), pieces.at[lax.div(s, 8), lax.rem(s, 8)], lsem.at[3])
    keep_rows = pltpu.make_async_copy(pieces.at[:, z], wo.at[s, :, z], lsem.at[2])

    def spread():
        keep_piece.start()
        for n in range(1, SHARDS):
            copy = part(n, piece(plane[n][0]), pieces.at[lax.div(s, 8), lax.rem(s, 8)], plane[n])
            copy.start()
            started.append(copy)

    senders = [(sid(xi, yi, ci), w) for xi in (x, xm, xp, xo) for yi in (yl, yp) for ci in (core, sib_core)]

    def deal():
        keep_piece.wait()
        for n in range(1, SHARDS):
            place = pieces.at[lax.div(senders[n][0], 8), lax.rem(senders[n][0], 8)]
            part(n, place, place, to_sib).wait_recv()
        keep_rows.start()
        for d in (4, 3, 5, 2, 6, 1, 7):
            copy = part(15 + d, pieces.at[:, ring[d]], wo.at[s, :, z], (s, wid(yh, ring[d])))
            copy.start()
            started.append(copy)

    def all_dealt():
        keep_rows.wait()
        for d in range(1, 8):
            place = wo.at[s, :, ring[8 - d]]
            part(15 + d, place, place, to_sib).wait_recv()

    spread()

    load_hidden.wait()

    def square(i, acc):
        block = hid[:, pl.ds(pl.multiple_of(i * BLOCK, BLOCK), BLOCK)].astype(f32)
        block = block * block
        return acc + (block[:, :128] + block[:, 128:256]) + (block[:, 256:384] + block[:, 384:])

    squares = lax.fori_loop(0, SHARDS, square, jnp.zeros((ROWS, 128), f32))
    inverse = lax.rsqrt(jnp.sum(squares, axis=1, keepdims=True) * (1.0 / 8192.0) + 1e-05)

    near_x(KV_WEIGHT)
    near_y(KV_WEIGHT)
    own_x(QUERY, wq_ref)
    opposite(KV_WEIGHT)
    own_y(QUERY, wq_ref)


    def scale(i, _):
        columns = pl.ds(pl.multiple_of(i * BLOCK, BLOCK), BLOCK)
        block = hid[:, columns].astype(f32) * inverse * gain_ref[columns].astype(f32)
        normed[i] = block.astype(bf16)
        return 0

    lax.fori_loop(0, SHARDS, scale, 0)
    corners(KV_WEIGHT)
    far(KV_WEIGHT)

    for p in range(8):
        from_sib(KV_WEIGHT, p)

    def project(i, acc):
        return acc + jnp.dot(normed[i], wkv[i], preferred_element_type=f32)

    raw = lax.fori_loop(0, SHARDS, project, jnp.zeros((ROWS, HEAD), f32))
    load_inner.wait()
    load_outer.wait()
    cosines = outer[0] * inner[0] - outer[1] * inner[1]
    sines = outer[1] * inner[0] + outer[0] * inner[1]

    def rotate(u):
        return u * cosines + pltpu.roll(u, HEAD // 2, 1) * sines

    rows_here = pl.ds(pl.multiple_of(s * ROWS, ROWS), ROWS)
    is_value = (lax.broadcasted_iota(jnp.int32, (ROWS, HEAD), 0) * 0 + par) == 1
    kv[par, rows_here] = jnp.where(is_value, raw, rotate(raw)).astype(bf16)
    pair = pltpu.make_async_remote_copy(
        src_ref=kv.at[par, rows_here], dst_ref=kv.at[par, rows_here], send_sem=xsend.at[0], recv_sem=xrecv.at[0],
        device_id=to_pair, device_id_type=MESH,
    )
    pair.start()
    started.append(pair)
    load_q.wait()

    def accumulate(shard, start=False):
        term = jnp.dot(normed[shard], wq[shard], preferred_element_type=f32)
        qacc[...] = term if start else qacc[...] + term

    accumulate(mine[0], True)
    pltpu.make_async_remote_copy(
        src_ref=kv.at[1 - par, rows_here], dst_ref=kv.at[1 - par, rows_here], send_sem=xsend.at[0],
        recv_sem=xrecv.at[0], device_id=to_pair, device_id_type=MESH,
    ).wait_recv()
    own_sends(KEYS, slot(KEYS, s))
    deal()
    near_x(QUERY)
    from_sib(QUERY, 0)
    accumulate(theirs[0])
    near_x(KEYS)
    near_y(KEYS)
    near_y(QUERY)
    accumulate(mine[1])
    accumulate(mine[2])
    accumulate(mine[3])
    for p in (1, 2, 3):
        from_sib(QUERY, p)
        accumulate(theirs[p])
    opposite(QUERY)
    opposite(KEYS)
    corners(KEYS)
    far(KEYS)
    all_dealt()
    own_sends(OUTPUT, wo.at[s])
    accumulate(mine[6])
    from_sib(QUERY, 6)
    accumulate(theirs[6])
    corners(QUERY)
    for p in (4, 5):
        accumulate(mine[p])
    far(QUERY)
    accumulate(mine[7])
    for p in (4, 5, 7):
        from_sib(QUERY, p)
        accumulate(theirs[p])
    for h in range(HEADS_HERE):
        qrot[h] = rotate(qacc[:, h * HEAD : (h + 1) * HEAD]).astype(bf16)
    for p in range(8):
        from_sib(KEYS, p)

    ones = jnp.ones((BLOCK, HEAD), bf16)

    def scores_of(h, block):
        rows = pl.ds(pl.multiple_of(block * BLOCK, BLOCK), BLOCK)
        return lax.dot_general(
            qrot[h], kv[0, rows], (((1,), (1,)), ((), ())), preferred_element_type=f32
        )

    def values_of(block):
        rows = pl.ds(pl.multiple_of(block * BLOCK, BLOCK), BLOCK)
        return jnp.concatenate([kv[1, rows], ones], axis=1)

    query_at = lax.broadcasted_iota(jnp.int32, (ROWS, BLOCK), 0) + core * ROWS
    allowed = lax.broadcasted_iota(jnp.int32, (ROWS, BLOCK), 1) <= query_at
    def hop(label, source, place, peer):
        copy = pltpu.make_async_remote_copy(
            src_ref=source, dst_ref=place, send_sem=rsend.at[label], recv_sem=rrecv.at[label],
            device_id=peer, device_id_type=MESH,
        )
        copy.start()
        started.append(copy)

    def landed(label, place):
        pltpu.make_async_remote_copy(
            src_ref=place, dst_ref=place, send_sem=rsend.at[label], recv_sem=rrecv.at[label],
            device_id=to_sib, device_id_type=MESH,
        ).wait_recv()

    def zplace(source, h, half=None):
        return heads.at[source, h] if half is None else heads.at[source, h, pl.ds(half * 128, 128)]

    def zsource(way, d):
        return lax.rem(z + 8 - d, 8) if way == 0 else lax.rem(z + d, 8)

    def zsend(h, way, d):
        place = zplace(zsource(way, d - 1), h, way if d == 4 else None)
        hop((h * 2 + way) * 4 + d - 1, place, place, (to_zp, to_zm)[way])

    def zland(h, way, d):
        landed((h * 2 + way) * 4 + d - 1, zplace(zsource(way, d), h, way if d == 4 else None))

    def zstep(first, d):
        for h in (first, first + 1):
            for way in range(2):
                zland(h, way, d)
                if d < 4:
                    zsend(h, way, d + 1)

    odd, doubles = lax.rem(chip, 2), lax.div(chip, 2)
    for pair_first in (0, 2):
        both = (pair_first, pair_first + 1)
        for h in both:
            scores = jnp.where(allowed, scores_of(h, chip), -1e30)
            high = jnp.max(scores, axis=1, keepdims=True)
            weights = jnp.exp2((scores - high) * SCORE_LOG2).astype(bf16)
            oacc[h] = jnp.dot(weights, values_of(chip), preferred_element_type=f32)
            macc[h] = jnp.broadcast_to(high, (ROWS, HEAD))

        def attend(first, width, both=both):
            blocks = range(width)
            values = [values_of(first + i) for i in blocks]
            for h in both:
                scores = [scores_of(h, first + i) for i in blocks]
                before = macc[h][:, :1]
                peak = scores[0]
                for more in scores[1:]:
                    peak = jnp.maximum(peak, more)
                high = jnp.maximum(before, jnp.max(peak, axis=1, keepdims=True))
                keep = jnp.exp2((before - high) * SCORE_LOG2)
                mixed = oacc[h] * keep
                for i in blocks:
                    weights = jnp.exp2((scores[i] - high) * SCORE_LOG2).astype(bf16)
                    mixed = mixed + jnp.dot(weights, values[i], preferred_element_type=f32)
                oacc[h] = mixed
                macc[h] = jnp.broadcast_to(high, (ROWS, HEAD))

        def attend_one(block, _):
            attend(block, 1)
            return 0

        def attend_two(i, _):
            attend(odd + 2 * i, 2)
            return 0

        lax.fori_loop(0, odd, attend_one, 0)
        lax.fori_loop(0, jnp.minimum(doubles, 2), attend_two, 0)
        if pair_first == 2:
            zstep(0, 1)
            near_x(OUTPUT)
            near_y(OUTPUT)
        lax.fori_loop(2, jnp.maximum(doubles, 2), attend_two, 0)
        for h in both:
            heads[z, h] = (oacc[h][:, :HEAD] / oacc[h][:, HEAD:]).astype(bf16)
            zsend(h, 0, 1)
            zsend(h, 1, 1)
    zstep(0, 2)
    zstep(2, 1)
    opposite(OUTPUT)
    zstep(0, 3)
    zstep(2, 2)
    zstep(0, 4)
    zstep(2, 3)
    zstep(2, 4)

    def columns_from(p, fresh):
        row, column = chips[p]
        place = row * 2 + column
        left = jnp.concatenate([heads[i, row] for i in range(8)], axis=1)
        for yi in range(2):
            right = jnp.concatenate(
                [wo[place * 2 + i, yi].reshape(8 * HEAD, HEAD) for i in range(2)], axis=1
            )
            term = jnp.dot(left, right, preferred_element_type=f32)
            tacc[yi, column] = term if fresh else tacc[yi, column] + term

    def hand_over(n, column):
        ysnd[column] = tacc[1 - yh, column].astype(bf16)
        hop(32 + n, ysnd.at[column], yrcv.at[column], to_yh)

    for p in (0, 2, 3):
        from_sib(OUTPUT, p)
        columns_from(p, p == 0)
    from_sib(OUTPUT, 6)
    columns_from(6, False)
    hand_over(0, yl)
    from_sib(OUTPUT, 1)
    columns_from(1, True)
    corners(OUTPUT)
    for p in (4, 5):
        from_sib(OUTPUT, p)
        columns_from(p, False)
    far(OUTPUT)
    from_sib(OUTPUT, 7)
    columns_from(7, False)
    hand_over(1, yp)
    for n, column in enumerate((yl, yp)):
        landed(32 + n, yrcv.at[column])
        at = pl.ds(pl.multiple_of(column * 256, 256), 256)
        wide = pl.ds(pl.multiple_of(w * BLOCK + column * 256, 256), 256)
        out_ref[:, at] = (hid[:, wide].astype(f32) + tacc[yh, column] + yrcv[column].astype(f32)).astype(bf16)
    for copy in started:
        copy.wait_send()


def local(hidden_states, norm_gain, query_weight, key_value_matrix, output_weight):
    tables = [jnp.asarray(t) for t in rope_constants()]
    anywhere = pl.BlockSpec(memory_space=pl.ANY)
    inside = pl.BlockSpec(memory_space=pltpu.VMEM)
    dma = pltpu.SemaphoreType.DMA
    return pl.pallas_call(
        body,
        out_shape=jax.ShapeDtypeStruct((ROWS, BLOCK), bf16),
        in_specs=[anywhere, inside, anywhere, anywhere, anywhere] + [anywhere] * 2,
        out_specs=inside,
        scratch_shapes=[
            pltpu.VMEM((2, ROWS, HEAD), f32),
            pltpu.VMEM((2, 1, HEAD), f32),
            pltpu.VMEM((ROWS, 8192), bf16),
            pltpu.VMEM((SHARDS, ROWS, BLOCK), bf16),
            pltpu.VMEM((SHARDS, BLOCK, HEAD), bf16),
            pltpu.VMEM((SHARDS, BLOCK, BLOCK), bf16),
            pltpu.VMEM((SHARDS, 2, 8, HEAD, HEAD), bf16),
            pltpu.VMEM((2, 8, HEAD, HEAD), bf16),
            pltpu.VMEM((2, SHARDS * ROWS, HEAD), bf16),
            pltpu.VMEM((ROWS, BLOCK), f32),
            pltpu.VMEM((HEADS_HERE, ROWS, HEAD), bf16),
            pltpu.VMEM((HEADS_HERE, ROWS, HEAD), f32),
            pltpu.VMEM((HEADS_HERE, ROWS, 2 * HEAD), f32),
            pltpu.VMEM((8, HEADS_HERE, ROWS, HEAD), bf16),
            pltpu.VMEM((2, 2, ROWS, 256), f32),
            pltpu.VMEM((2, ROWS, 256), bf16),
            pltpu.VMEM((2, ROWS, 256), bf16),
            dma((4, 16)),
            dma((4, 16)),
            dma((34,)),
            dma((34,)),
            dma((23,)),
            dma((23,)),
            dma((1,)),
            dma((1,)),
            dma((6,)),
        ],
        compiler_params=pltpu.CompilerParams(
            collective_id=0, has_side_effects=True, vmem_limit_bytes=56 * 1024 * 1024
        ),
    )(hidden_states, norm_gain, query_weight, key_value_matrix, output_weight, *tables)


def solution(mesh):
    in_specs = (P("seq", None), P(), P("seq", "wt"), P("seq", None), P("wt", "seq"))
    return jax.shard_map(local, mesh=mesh, in_specs=in_specs, out_specs=P("seq", "wt"), check_vma=False)
```

```python
import math

import jax
import jax.numpy as jnp
import numpy as np
from jax import lax
from jax.experimental import pallas as pl
from jax.experimental.pallas import tpu as pltpu
from jax.sharding import PartitionSpec as P

MESH = pl.DeviceIdType.MESH
HEAD = 128
ROWS = 256
SHARDS = 16
BLOCK = 512
HEADS_HERE = 4
SCORE_LOG2 = math.log2(math.e) / math.sqrt(HEAD)
KV_WEIGHT, QUERY, OUTPUT, KEYS = 0, 1, 2, 3
MAIN, PART = 2, 3
f32 = jnp.float32
bf16 = jnp.bfloat16


def rope_constants():
    inverse = 500000.0 ** (-np.arange(HEAD // 2) * 2.0 / HEAD)
    wide = np.concatenate([inverse, inverse])
    sign = np.concatenate([-np.ones(HEAD // 2), np.ones(HEAD // 2)])
    inner = np.arange(ROWS)[:, None] * wide[None, :]
    outer = (np.arange(SHARDS) * ROWS)[:, None] * wide[None, :]
    outer = outer[:, None, :]
    return [np.stack([np.cos(t), np.sin(t) * sign]).astype(np.float32) for t in (inner, outer)]


def body(
    hidden_ref, gain_ref, wq_ref, wkv_ref, wo_ref, inner_ref, outer_ref, out_ref,
    inner, outer,
    hid, normed, wkv, wq, wo, pieces, kv, qacc, qrot, macc, oacc, heads, tacc, ysnd, yrcv,
    gsend, grecv, rsend, rrecv, dsend, drecv, xsend, xrecv, lsem,
):
    s = lax.axis_index("seq")
    w = lax.axis_index("wt")
    x, yl, core = lax.div(s, 4), lax.rem(lax.div(s, 2), 2), lax.rem(s, 2)
    yh, z = lax.div(w, 8), lax.rem(w, 8)
    xp, xm, xo = lax.rem(x + 1, 4), lax.rem(x + 3, 4), lax.rem(x + 2, 4)
    yp, sib_core = 1 - yl, 1 - core
    par = lax.rem(z, 2)
    chip = lax.div(s, 2)

    def sid(xi, yi, ci):
        return (xi * 2 + yi) * 2 + ci

    def wid(yi, zi):
        return yi * 8 + zi

    to_xp, to_xm = (sid(xp, yl, core), w), (sid(xm, yl, core), w)
    to_y, to_sib = (sid(x, yp, core), w), (sid(x, yl, sib_core), w)
    to_zp, to_zm = (s, wid(yh, lax.rem(z + 1, 8))), (s, wid(yh, lax.rem(z + 7, 8)))
    to_yh = (s, wid(1 - yh, z))
    to_pair = (s, wid(yh, z + 1 - 2 * par))

    barrier = pltpu.get_barrier_semaphore()
    for peer in (to_xp, to_xm, to_y, to_sib, to_zp, to_zm, to_yh):
        pl.semaphore_signal(barrier, inc=1, device_id=peer, device_id_type=MESH)
    plane = [(sid(xi, yi, ci), w) for xi in (x, xp, xm, xo) for yi in (yl, yp) for ci in (core, sib_core)]
    ring = [lax.rem(z + d, 8) for d in range(8)]
    others = [peer for n, peer in enumerate(plane) if n not in (0, 1, 2, 4, 8)]
    others += [(s, wid(yh, ring[d])) for d in range(2, 7)]
    for peer in others:
        pl.semaphore_signal(barrier, inc=1, device_id=peer, device_id_type=MESH)

    first = pltpu.make_async_copy(
        wkv_ref.at[:, pl.ds(pl.multiple_of(w * HEAD, HEAD), HEAD)], wkv.at[s], lsem.at[0]
    )
    load_hidden = pltpu.make_async_copy(hidden_ref, hid, lsem.at[1])
    load_q = pltpu.make_async_copy(wq_ref, wq.at[s], lsem.at[2])
    load_inner = pltpu.make_async_copy(inner_ref, inner, lsem.at[4])
    load_outer = pltpu.make_async_copy(outer_ref.at[:, s], outer, lsem.at[5])
    first.start()
    load_hidden.start()
    load_q.start()
    load_inner.start()
    load_outer.start()
    pl.semaphore_wait(barrier, 7 + len(others))

    stores = {KV_WEIGHT: wkv, QUERY: wq, OUTPUT: wo}

    def slot(k, shard, half=None):
        if k == KEYS:
            rows = pl.ds(pl.multiple_of(shard * ROWS, ROWS), ROWS)
            return kv.at[:, rows] if half is None else kv.at[half, rows]
        if half is None:
            return stores[k].at[shard]
        if half in (MAIN, PART):
            if k == OUTPUT:
                return wo.at[shard, :, pl.ds(0, 7) if half == MAIN else pl.ds(7, 1)]
            return stores[k].at[shard, pl.ds(0, 448) if half == MAIN else pl.ds(448, 64)]
        if k == OUTPUT:
            return wo.at[shard, half]
        return stores[k].at[shard, pl.ds(half * 256, 256)]

    started = []

    def send(k, label, source, place, peer):
        copy = pltpu.make_async_remote_copy(
            src_ref=source, dst_ref=place, send_sem=gsend.at[k, label], recv_sem=grecv.at[k, label],
            device_id=peer, device_id_type=MESH,
        )
        copy.start()
        started.append(copy)

    def forward(k, label, shard, peer, half=None):
        send(k, label, slot(k, shard, half), slot(k, shard, half), peer)

    def arrive(k, label, shard, half=None):
        place = slot(k, shard, half)
        pltpu.make_async_remote_copy(
            src_ref=place, dst_ref=place, send_sem=gsend.at[k, label], recv_sem=grecv.at[k, label],
            device_id=to_sib, device_id_type=MESH,
        ).wait_recv()

    chips = [(x, yl), (x, yp), (xm, yl), (xp, yl), (xm, yp), (xp, yp), (xo, yl), (xo, yp)]
    mine = [sid(a, b, core) for a, b in chips]
    theirs = [sid(a, b, sib_core) for a, b in chips]
    sib_label = [3, 9, 10, 11, 12, 13, 14, 15]

    def own_x(k, source):
        for label, peer in ((0, to_xp), (1, to_xm), (3, to_sib)):
            send(k, label, source, slot(k, s), peer)

    def own_y(k, source):
        send(k, 2, source, slot(k, s), to_y)

    def own_sends(k, source):
        own_x(k, source)
        own_y(k, source)

    def near_x(k):
        for label, p, peer in ((0, 2, to_xp), (1, 3, to_xm)):
            arrive(k, label, mine[p])
            forward(k, 6 + label, mine[p], peer, label)
            if k in (QUERY, OUTPUT):
                forward(k, 16 + label, mine[p], to_y, PART)
        for p in (2, 3):
            forward(k, sib_label[p], mine[p], to_sib)

    def near_y(k):
        arrive(k, 2, mine[1])
        main = MAIN if k in (QUERY, OUTPUT) else None
        forward(k, 4, mine[1], to_xp, main)
        forward(k, 5, mine[1], to_xm, main)
        forward(k, sib_label[1], mine[1], to_sib)

    def opposite(k):
        arrive(k, 6, mine[6], 0)
        arrive(k, 7, mine[6], 1)
        forward(k, 8, mine[6], to_y)
        forward(k, sib_label[6], mine[6], to_sib)

    def corners(k):
        for label, p in ((4, 4), (5, 5)):
            if k in (QUERY, OUTPUT):
                arrive(k, label, mine[p], MAIN)
                arrive(k, label + 12, mine[p], PART)
            else:
                arrive(k, label, mine[p])
            forward(k, sib_label[p], mine[p], to_sib)

    def far(k):
        arrive(k, 8, mine[7])
        forward(k, sib_label[7], mine[7], to_sib)

    def from_sib(k, p):
        arrive(k, sib_label[p], theirs[p])

    first.wait()
    own_sends(KV_WEIGHT, wkv.at[s])

    def piece(p):
        return wo_ref.at[
            pl.ds(pl.multiple_of(lax.div(p, 4) * HEAD, HEAD), HEAD), pl.ds(pl.multiple_of(lax.rem(p, 4) * HEAD, HEAD), HEAD)
        ]

    def part(label, source, place, peer):
        copy = pltpu.make_async_remote_copy(
            src_ref=source, dst_ref=place, send_sem=dsend.at[label], recv_sem=drecv.at[label],
            device_id=peer, device_id_type=MESH,
        )
        return copy

    keep_piece = pltpu.make_async_copy(piece(s), pieces.at[lax.div(s, 8), lax.rem(s, 8)], lsem.at[3])
    keep_rows = pltpu.make_async_copy(pieces.at[:, z], wo.at[s, :, z], lsem.at[2])

    def spread():
        keep_piece.start()
        for n in range(1, SHARDS):
            copy = part(n, piece(plane[n][0]), pieces.at[lax.div(s, 8), lax.rem(s, 8)], plane[n])
            copy.start()
            started.append(copy)

    senders = [(sid(xi, yi, ci), w) for xi in (x, xm, xp, xo) for yi in (yl, yp) for ci in (core, sib_core)]

    def deal():
        keep_piece.wait()
        for n in range(1, SHARDS):
            place = pieces.at[lax.div(senders[n][0], 8), lax.rem(senders[n][0], 8)]
            part(n, place, place, to_sib).wait_recv()
        keep_rows.start()
        for d in (4, 3, 5, 2, 6, 1, 7):
            copy = part(15 + d, pieces.at[:, ring[d]], wo.at[s, :, z], (s, wid(yh, ring[d])))
            copy.start()
            started.append(copy)

    def all_dealt():
        keep_rows.wait()
        for d in range(1, 8):
            place = wo.at[s, :, ring[8 - d]]
            part(15 + d, place, place, to_sib).wait_recv()

    spread()

    load_hidden.wait()

    def square(i, acc):
        block = hid[:, pl.ds(pl.multiple_of(i * BLOCK, BLOCK), BLOCK)].astype(f32)
        block = block * block
        return acc + (block[:, :128] + block[:, 128:256]) + (block[:, 256:384] + block[:, 384:])

    squares = lax.fori_loop(0, SHARDS, square, jnp.zeros((ROWS, 128), f32))
    inverse = lax.rsqrt(jnp.sum(squares, axis=1, keepdims=True) * (1.0 / 8192.0) + 1e-05)

    near_x(KV_WEIGHT)
    near_y(KV_WEIGHT)
    own_x(QUERY, wq_ref)
    opposite(KV_WEIGHT)
    own_y(QUERY, wq_ref)


    def scale(i, _):
        columns = pl.ds(pl.multiple_of(i * BLOCK, BLOCK), BLOCK)
        block = hid[:, columns].astype(f32) * inverse * gain_ref[columns].astype(f32)
        normed[i] = block.astype(bf16)
        return 0

    lax.fori_loop(0, SHARDS, scale, 0)
    corners(KV_WEIGHT)
    far(KV_WEIGHT)

    for p in range(8):
        from_sib(KV_WEIGHT, p)

    def project(i, acc):
        return acc + jnp.dot(normed[i], wkv[i], preferred_element_type=f32)

    raw = lax.fori_loop(0, SHARDS, project, jnp.zeros((ROWS, HEAD), f32))
    load_inner.wait()
    load_outer.wait()
    cosines = outer[0] * inner[0] - outer[1] * inner[1]
    sines = outer[1] * inner[0] + outer[0] * inner[1]

    def rotate(u):
        return u * cosines + pltpu.roll(u, HEAD // 2, 1) * sines

    rows_here = pl.ds(pl.multiple_of(s * ROWS, ROWS), ROWS)
    is_value = (lax.broadcasted_iota(jnp.int32, (ROWS, HEAD), 0) * 0 + par) == 1
    kv[par, rows_here] = jnp.where(is_value, raw, rotate(raw)).astype(bf16)
    pair = pltpu.make_async_remote_copy(
        src_ref=kv.at[par, rows_here], dst_ref=kv.at[par, rows_here], send_sem=xsend.at[0], recv_sem=xrecv.at[0],
        device_id=to_pair, device_id_type=MESH,
    )
    pair.start()
    started.append(pair)
    load_q.wait()

    def accumulate(shard, start=False):
        term = jnp.dot(normed[shard], wq[shard], preferred_element_type=f32)
        qacc[...] = term if start else qacc[...] + term

    accumulate(mine[0], True)
    pltpu.make_async_remote_copy(
        src_ref=kv.at[1 - par, rows_here], dst_ref=kv.at[1 - par, rows_here], send_sem=xsend.at[0],
        recv_sem=xrecv.at[0], device_id=to_pair, device_id_type=MESH,
    ).wait_recv()
    own_sends(KEYS, slot(KEYS, s))
    deal()
    near_x(QUERY)
    from_sib(QUERY, 0)
    accumulate(theirs[0])
    near_x(KEYS)
    near_y(KEYS)
    near_y(QUERY)
    accumulate(mine[1])
    accumulate(mine[2])
    accumulate(mine[3])
    for p in (1, 2, 3):
        from_sib(QUERY, p)
        accumulate(theirs[p])
    opposite(KEYS)
    opposite(QUERY)
    corners(KEYS)
    all_dealt()
    own_sends(OUTPUT, wo.at[s])
    far(KEYS)
    accumulate(mine[6])
    from_sib(QUERY, 6)
    accumulate(theirs[6])
    corners(QUERY)
    for p in (4, 5):
        accumulate(mine[p])
    far(QUERY)
    accumulate(mine[7])
    for p in (4, 5, 7):
        from_sib(QUERY, p)
        accumulate(theirs[p])
    for h in range(HEADS_HERE):
        qrot[h] = rotate(qacc[:, h * HEAD : (h + 1) * HEAD]).astype(bf16)
    for p in range(8):
        from_sib(KEYS, p)

    ones = jnp.ones((BLOCK, HEAD), bf16)

    turns = (x, xm, xp, xo)

    def scores_of(h, block):
        rows = pl.ds(pl.multiple_of(block * BLOCK, BLOCK), BLOCK)
        return lax.dot_general(
            qrot[turns[h]], kv[0, rows], (((1,), (1,)), ((), ())), preferred_element_type=f32
        )

    def values_of(block):
        rows = pl.ds(pl.multiple_of(block * BLOCK, BLOCK), BLOCK)
        return jnp.concatenate([kv[1, rows], ones], axis=1)

    query_at = lax.broadcasted_iota(jnp.int32, (ROWS, BLOCK), 0) + core * ROWS
    allowed = lax.broadcasted_iota(jnp.int32, (ROWS, BLOCK), 1) <= query_at
    def hop(label, source, place, peer):
        copy = pltpu.make_async_remote_copy(
            src_ref=source, dst_ref=place, send_sem=rsend.at[label], recv_sem=rrecv.at[label],
            device_id=peer, device_id_type=MESH,
        )
        copy.start()
        started.append(copy)

    def landed(label, place):
        pltpu.make_async_remote_copy(
            src_ref=place, dst_ref=place, send_sem=rsend.at[label], recv_sem=rrecv.at[label],
            device_id=to_sib, device_id_type=MESH,
        ).wait_recv()

    def zplace(source, h, half=None):
        whole = heads.at[source, turns[h]]
        return whole if half is None else heads.at[source, turns[h], pl.ds(half * 128, 128)]

    def zsource(way, d):
        return lax.rem(z + 8 - d, 8) if way == 0 else lax.rem(z + d, 8)

    def zsend(h, way, d):
        place = zplace(zsource(way, d - 1), h, way if d == 4 else None)
        hop((h * 2 + way) * 4 + d - 1, place, place, (to_zp, to_zm)[way])

    def zland(h, way, d):
        landed((h * 2 + way) * 4 + d - 1, zplace(zsource(way, d), h, way if d == 4 else None))

    def zstep(first, d):
        for h in (first, first + 1):
            for way in range(2):
                zland(h, way, d)
                if d < 4:
                    zsend(h, way, d + 1)

    odd, doubles = lax.rem(chip, 2), lax.div(chip, 2)
    for pair_first in (0, 2):
        both = (pair_first, pair_first + 1)
        for h in both:
            scores = jnp.where(allowed, scores_of(h, chip), -1e30)
            high = jnp.max(scores, axis=1, keepdims=True)
            weights = jnp.exp2((scores - high) * SCORE_LOG2).astype(bf16)
            oacc[h] = jnp.dot(weights, values_of(chip), preferred_element_type=f32)
            macc[h] = jnp.broadcast_to(high, (ROWS, HEAD))

        def attend(first, width, both=both):
            blocks = range(width)
            values = [values_of(first + i) for i in blocks]
            for h in both:
                scores = [scores_of(h, first + i) for i in blocks]
                before = macc[h][:, :1]
                peak = scores[0]
                for more in scores[1:]:
                    peak = jnp.maximum(peak, more)
                high = jnp.maximum(before, jnp.max(peak, axis=1, keepdims=True))
                keep = jnp.exp2((before - high) * SCORE_LOG2)
                mixed = oacc[h] * keep
                for i in blocks:
                    weights = jnp.exp2((scores[i] - high) * SCORE_LOG2).astype(bf16)
                    mixed = mixed + jnp.dot(weights, values[i], preferred_element_type=f32)
                oacc[h] = mixed
                macc[h] = jnp.broadcast_to(high, (ROWS, HEAD))

        def attend_one(block, _):
            attend(block, 1)
            return 0

        def attend_two(i, _):
            attend(odd + 2 * i, 2)
            return 0

        lax.fori_loop(0, odd, attend_one, 0)
        lax.fori_loop(0, jnp.minimum(doubles, 2), attend_two, 0)
        if pair_first == 2:
            zstep(0, 1)
            near_x(OUTPUT)
            near_y(OUTPUT)
        lax.fori_loop(2, jnp.maximum(doubles, 2), attend_two, 0)
        for h in both:
            heads[z, turns[h]] = (oacc[h][:, :HEAD] / oacc[h][:, HEAD:]).astype(bf16)
            zsend(h, 0, 1)
            zsend(h, 1, 1)
    def columns_from(p, fresh):
        row, column = chips[p]
        place = row * 2 + column
        left = jnp.concatenate([heads[i, row] for i in range(8)], axis=1)
        for yi in range(2):
            right = jnp.concatenate(
                [wo[place * 2 + i, yi].reshape(8 * HEAD, HEAD) for i in range(2)], axis=1
            )
            term = jnp.dot(left, right, preferred_element_type=f32)
            tacc[yi, column] = term if fresh else tacc[yi, column] + term

    zstep(0, 2)
    zstep(2, 1)
    opposite(OUTPUT)
    zstep(0, 3)
    zstep(2, 2)
    zstep(0, 4)
    zstep(2, 3)
    for p, fresh in ((0, True), (2, False), (1, True)):
        from_sib(OUTPUT, p)
        columns_from(p, fresh)
    zstep(2, 4)

    def hand_over(n, column):
        ysnd[column] = tacc[1 - yh, column].astype(bf16)
        hop(32 + n, ysnd.at[column], yrcv.at[column], to_yh)

    for p in (3, 6):
        from_sib(OUTPUT, p)
        columns_from(p, False)
    hand_over(0, yl)
    corners(OUTPUT)
    for p in (4, 5):
        from_sib(OUTPUT, p)
        columns_from(p, False)
    far(OUTPUT)
    from_sib(OUTPUT, 7)
    columns_from(7, False)
    hand_over(1, yp)
    for n, column in enumerate((yl, yp)):
        landed(32 + n, yrcv.at[column])
        at = pl.ds(pl.multiple_of(column * 256, 256), 256)
        wide = pl.ds(pl.multiple_of(w * BLOCK + column * 256, 256), 256)
        out_ref[:, at] = (hid[:, wide].astype(f32) + tacc[yh, column] + yrcv[column].astype(f32)).astype(bf16)
    for copy in started:
        copy.wait_send()


def local(hidden_states, norm_gain, query_weight, key_value_matrix, output_weight):
    tables = [jnp.asarray(t) for t in rope_constants()]
    anywhere = pl.BlockSpec(memory_space=pl.ANY)
    inside = pl.BlockSpec(memory_space=pltpu.VMEM)
    dma = pltpu.SemaphoreType.DMA
    return pl.pallas_call(
        body,
        out_shape=jax.ShapeDtypeStruct((ROWS, BLOCK), bf16),
        in_specs=[anywhere, inside, anywhere, anywhere, anywhere] + [anywhere] * 2,
        out_specs=inside,
        scratch_shapes=[
            pltpu.VMEM((2, ROWS, HEAD), f32),
            pltpu.VMEM((2, 1, HEAD), f32),
            pltpu.VMEM((ROWS, 8192), bf16),
            pltpu.VMEM((SHARDS, ROWS, BLOCK), bf16),
            pltpu.VMEM((SHARDS, BLOCK, HEAD), bf16),
            pltpu.VMEM((SHARDS, BLOCK, BLOCK), bf16),
            pltpu.VMEM((SHARDS, 2, 8, HEAD, HEAD), bf16),
            pltpu.VMEM((2, 8, HEAD, HEAD), bf16),
            pltpu.VMEM((2, SHARDS * ROWS, HEAD), bf16),
            pltpu.VMEM((ROWS, BLOCK), f32),
            pltpu.VMEM((HEADS_HERE, ROWS, HEAD), bf16),
            pltpu.VMEM((HEADS_HERE, ROWS, HEAD), f32),
            pltpu.VMEM((HEADS_HERE, ROWS, 2 * HEAD), f32),
            pltpu.VMEM((8, HEADS_HERE, ROWS, HEAD), bf16),
            pltpu.VMEM((2, 2, ROWS, 256), f32),
            pltpu.VMEM((2, ROWS, 256), bf16),
            pltpu.VMEM((2, ROWS, 256), bf16),
            dma((4, 18)),
            dma((4, 18)),
            dma((34,)),
            dma((34,)),
            dma((23,)),
            dma((23,)),
            dma((1,)),
            dma((1,)),
            dma((6,)),
        ],
        compiler_params=pltpu.CompilerParams(
            collective_id=0, has_side_effects=True, vmem_limit_bytes=56 * 1024 * 1024
        ),
    )(hidden_states, norm_gain, query_weight, key_value_matrix, output_weight, *tables)


def solution(mesh):
    in_specs = (P("seq", None), P(), P("seq", "wt"), P("seq", None), P("wt", "seq"))
    return jax.shard_map(local, mesh=mesh, in_specs=in_specs, out_specs=P("seq", "wt"), check_vma=False)
```

```python
import math

import jax
import jax.numpy as jnp
import numpy as np
from jax import lax
from jax.experimental import pallas as pl
from jax.experimental.pallas import tpu as pltpu
from jax.sharding import PartitionSpec as P

MESH = pl.DeviceIdType.MESH
HEAD = 128
ROWS = 256
SHARDS = 16
BLOCK = 512
HEADS_HERE = 4
SCORE_LOG2 = math.log2(math.e) / math.sqrt(HEAD)
KV_WEIGHT, QUERY, OUTPUT, KEYS = 0, 1, 2, 3
MAIN, PART = 2, 3
f32 = jnp.float32
bf16 = jnp.bfloat16


def rope_constants():
    inverse = 500000.0 ** (-np.arange(HEAD // 2) * 2.0 / HEAD)
    wide = np.concatenate([inverse, inverse])
    sign = np.concatenate([-np.ones(HEAD // 2), np.ones(HEAD // 2)])
    inner = np.arange(ROWS)[:, None] * wide[None, :]
    outer = (np.arange(SHARDS) * ROWS)[:, None] * wide[None, :]
    outer = outer[:, None, :]
    return [np.stack([np.cos(t), np.sin(t) * sign]).astype(np.float32) for t in (inner, outer)]


def body(
    hidden_ref, gain_ref, wq_ref, wkv_ref, wo_ref, inner_ref, outer_ref, out_ref,
    inner, outer,
    hid, normed, wkv, wq, wo, pieces, kv, qacc, qrot, macc, oacc, heads, tacc, ysnd, yrcv,
    gsend, grecv, rsend, rrecv, dsend, drecv, xsend, xrecv, lsem,
):
    s = lax.axis_index("seq")
    w = lax.axis_index("wt")
    x, yl, core = lax.div(s, 4), lax.rem(lax.div(s, 2), 2), lax.rem(s, 2)
    yh, z = lax.div(w, 8), lax.rem(w, 8)
    xp, xm, xo = lax.rem(x + 1, 4), lax.rem(x + 3, 4), lax.rem(x + 2, 4)
    yp, sib_core = 1 - yl, 1 - core
    par = lax.rem(z, 2)
    chip = lax.div(s, 2)

    def sid(xi, yi, ci):
        return (xi * 2 + yi) * 2 + ci

    def wid(yi, zi):
        return yi * 8 + zi

    to_xp, to_xm = (sid(xp, yl, core), w), (sid(xm, yl, core), w)
    to_y, to_sib = (sid(x, yp, core), w), (sid(x, yl, sib_core), w)
    to_zp, to_zm = (s, wid(yh, lax.rem(z + 1, 8))), (s, wid(yh, lax.rem(z + 7, 8)))
    to_yh = (s, wid(1 - yh, z))
    to_pair = (s, wid(yh, z + 1 - 2 * par))

    barrier = pltpu.get_barrier_semaphore()
    for peer in (to_xp, to_xm, to_y, to_sib, to_zp, to_zm, to_yh):
        pl.semaphore_signal(barrier, inc=1, device_id=peer, device_id_type=MESH)
    plane = [(sid(xi, yi, ci), w) for xi in (x, xp, xm, xo) for yi in (yl, yp) for ci in (core, sib_core)]
    ring = [lax.rem(z + d, 8) for d in range(8)]
    others = [peer for n, peer in enumerate(plane) if n not in (0, 1, 2, 4, 8)]
    others += [(s, wid(yh, ring[d])) for d in range(2, 7)]
    for peer in others:
        pl.semaphore_signal(barrier, inc=1, device_id=peer, device_id_type=MESH)

    first = pltpu.make_async_copy(
        wkv_ref.at[:, pl.ds(pl.multiple_of(w * HEAD, HEAD), HEAD)], wkv.at[s], lsem.at[0]
    )
    load_hidden = pltpu.make_async_copy(hidden_ref, hid, lsem.at[1])
    load_q = pltpu.make_async_copy(wq_ref, wq.at[s], lsem.at[2])
    load_inner = pltpu.make_async_copy(inner_ref, inner, lsem.at[4])
    load_outer = pltpu.make_async_copy(outer_ref.at[:, s], outer, lsem.at[5])
    first.start()
    load_hidden.start()
    load_q.start()
    load_inner.start()
    load_outer.start()
    pl.semaphore_wait(barrier, 7 + len(others))

    stores = {KV_WEIGHT: wkv, QUERY: wq, OUTPUT: wo}

    def slot(k, shard, half=None):
        if k == KEYS:
            rows = pl.ds(pl.multiple_of(shard * ROWS, ROWS), ROWS)
            return kv.at[:, rows] if half is None else kv.at[half, rows]
        if half is None:
            return stores[k].at[shard]
        if half in (MAIN, PART):
            if k == OUTPUT:
                return wo.at[shard, :, pl.ds(0, 7) if half == MAIN else pl.ds(7, 1)]
            return stores[k].at[shard, pl.ds(0, 448) if half == MAIN else pl.ds(448, 64)]
        if k == OUTPUT:
            return wo.at[shard, half]
        return stores[k].at[shard, pl.ds(half * 256, 256)]

    started = []

    def send(k, label, source, place, peer):
        copy = pltpu.make_async_remote_copy(
            src_ref=source, dst_ref=place, send_sem=gsend.at[k, label], recv_sem=grecv.at[k, label],
            device_id=peer, device_id_type=MESH,
        )
        copy.start()
        started.append(copy)

    def forward(k, label, shard, peer, half=None):
        send(k, label, slot(k, shard, half), slot(k, shard, half), peer)

    def arrive(k, label, shard, half=None):
        place = slot(k, shard, half)
        pltpu.make_async_remote_copy(
            src_ref=place, dst_ref=place, send_sem=gsend.at[k, label], recv_sem=grecv.at[k, label],
            device_id=to_sib, device_id_type=MESH,
        ).wait_recv()

    chips = [(x, yl), (x, yp), (xm, yl), (xp, yl), (xm, yp), (xp, yp), (xo, yl), (xo, yp)]
    mine = [sid(a, b, core) for a, b in chips]
    theirs = [sid(a, b, sib_core) for a, b in chips]
    sib_label = [3, 9, 10, 11, 12, 13, 14, 15]

    def own_x(k, source):
        for label, peer in ((0, to_xp), (1, to_xm), (3, to_sib)):
            send(k, label, source, slot(k, s), peer)

    def own_y(k, source):
        send(k, 2, source, slot(k, s), to_y)

    def own_sends(k, source):
        own_x(k, source)
        own_y(k, source)

    def near_x(k):
        for label, p, peer in ((0, 2, to_xp), (1, 3, to_xm)):
            arrive(k, label, mine[p])
            forward(k, 6 + label, mine[p], peer, label)
            if k in (QUERY, OUTPUT):
                forward(k, 16 + label, mine[p], to_y, PART)
        for p in (2, 3):
            forward(k, sib_label[p], mine[p], to_sib)

    def near_y(k):
        arrive(k, 2, mine[1])
        main = MAIN if k in (QUERY, OUTPUT) else None
        forward(k, 4, mine[1], to_xp, main)
        forward(k, 5, mine[1], to_xm, main)
        forward(k, sib_label[1], mine[1], to_sib)

    def opposite(k):
        arrive(k, 6, mine[6], 0)
        arrive(k, 7, mine[6], 1)
        forward(k, 8, mine[6], to_y)
        forward(k, sib_label[6], mine[6], to_sib)

    def corners(k):
        for label, p in ((4, 4), (5, 5)):
            if k in (QUERY, OUTPUT):
                arrive(k, label, mine[p], MAIN)
                arrive(k, label + 12, mine[p], PART)
            else:
                arrive(k, label, mine[p])
            forward(k, sib_label[p], mine[p], to_sib)

    def far(k):
        arrive(k, 8, mine[7])
        forward(k, sib_label[7], mine[7], to_sib)

    def from_sib(k, p):
        arrive(k, sib_label[p], theirs[p])

    first.wait()
    own_sends(KV_WEIGHT, wkv.at[s])

    def piece(p):
        return wo_ref.at[
            pl.ds(pl.multiple_of(lax.div(p, 4) * HEAD, HEAD), HEAD), pl.ds(pl.multiple_of(lax.rem(p, 4) * HEAD, HEAD), HEAD)
        ]

    def part(label, source, place, peer):
        copy = pltpu.make_async_remote_copy(
            src_ref=source, dst_ref=place, send_sem=dsend.at[label], recv_sem=drecv.at[label],
            device_id=peer, device_id_type=MESH,
        )
        return copy

    keep_piece = pltpu.make_async_copy(piece(s), pieces.at[lax.div(s, 8), lax.rem(s, 8)], lsem.at[3])
    keep_rows = pltpu.make_async_copy(pieces.at[:, z], wo.at[s, :, z], lsem.at[2])

    def spread():
        keep_piece.start()
        for n in range(1, SHARDS):
            copy = part(n, piece(plane[n][0]), pieces.at[lax.div(s, 8), lax.rem(s, 8)], plane[n])
            copy.start()
            started.append(copy)

    senders = [(sid(xi, yi, ci), w) for xi in (x, xm, xp, xo) for yi in (yl, yp) for ci in (core, sib_core)]

    def deal():
        keep_piece.wait()
        for n in range(1, SHARDS):
            place = pieces.at[lax.div(senders[n][0], 8), lax.rem(senders[n][0], 8)]
            part(n, place, place, to_sib).wait_recv()
        keep_rows.start()
        for d in (4, 3, 5, 2, 6, 1, 7):
            copy = part(15 + d, pieces.at[:, ring[d]], wo.at[s, :, z], (s, wid(yh, ring[d])))
            copy.start()
            started.append(copy)

    def all_dealt():
        keep_rows.wait()
        for d in range(1, 8):
            place = wo.at[s, :, ring[8 - d]]
            part(15 + d, place, place, to_sib).wait_recv()

    spread()

    load_hidden.wait()

    def square(i, acc):
        block = hid[:, pl.ds(pl.multiple_of(i * BLOCK, BLOCK), BLOCK)].astype(f32)
        block = block * block
        return acc + (block[:, :128] + block[:, 128:256]) + (block[:, 256:384] + block[:, 384:])

    squares = lax.fori_loop(0, SHARDS, square, jnp.zeros((ROWS, 128), f32))
    inverse = lax.rsqrt(jnp.sum(squares, axis=1, keepdims=True) * (1.0 / 8192.0) + 1e-05)

    near_x(KV_WEIGHT)
    near_y(KV_WEIGHT)
    own_x(QUERY, wq_ref)
    opposite(KV_WEIGHT)
    own_y(QUERY, wq_ref)


    def scale(i, _):
        columns = pl.ds(pl.multiple_of(i * BLOCK, BLOCK), BLOCK)
        block = hid[:, columns].astype(f32) * inverse * gain_ref[columns].astype(f32)
        normed[i] = block.astype(bf16)
        return 0

    lax.fori_loop(0, SHARDS, scale, 0)
    corners(KV_WEIGHT)
    far(KV_WEIGHT)

    for p in range(8):
        from_sib(KV_WEIGHT, p)

    def project(i, acc):
        return acc + jnp.dot(normed[i], wkv[i], preferred_element_type=f32)

    raw = lax.fori_loop(0, SHARDS, project, jnp.zeros((ROWS, HEAD), f32))
    load_inner.wait()
    load_outer.wait()
    cosines = outer[0] * inner[0] - outer[1] * inner[1]
    sines = outer[1] * inner[0] + outer[0] * inner[1]

    def rotate(u):
        return u * cosines + pltpu.roll(u, HEAD // 2, 1) * sines

    rows_here = pl.ds(pl.multiple_of(s * ROWS, ROWS), ROWS)
    is_value = (lax.broadcasted_iota(jnp.int32, (ROWS, HEAD), 0) * 0 + par) == 1
    kv[par, rows_here] = jnp.where(is_value, raw, rotate(raw)).astype(bf16)
    pair = pltpu.make_async_remote_copy(
        src_ref=kv.at[par, rows_here], dst_ref=kv.at[par, rows_here], send_sem=xsend.at[0], recv_sem=xrecv.at[0],
        device_id=to_pair, device_id_type=MESH,
    )
    pair.start()
    started.append(pair)
    load_q.wait()

    def accumulate(shard, start=False):
        term = jnp.dot(normed[shard], wq[shard], preferred_element_type=f32)
        qacc[...] = term if start else qacc[...] + term

    accumulate(mine[0], True)
    pltpu.make_async_remote_copy(
        src_ref=kv.at[1 - par, rows_here], dst_ref=kv.at[1 - par, rows_here], send_sem=xsend.at[0],
        recv_sem=xrecv.at[0], device_id=to_pair, device_id_type=MESH,
    ).wait_recv()
    own_sends(KEYS, slot(KEYS, s))
    deal()
    near_x(QUERY)
    from_sib(QUERY, 0)
    accumulate(theirs[0])
    near_x(KEYS)
    near_y(KEYS)
    near_y(QUERY)
    accumulate(mine[1])
    accumulate(mine[2])
    accumulate(mine[3])
    for p in (1, 2, 3):
        from_sib(QUERY, p)
        accumulate(theirs[p])
    opposite(KEYS)
    opposite(QUERY)
    corners(KEYS)
    all_dealt()
    own_sends(OUTPUT, wo.at[s])
    far(KEYS)
    accumulate(mine[6])
    from_sib(QUERY, 6)
    accumulate(theirs[6])
    corners(QUERY)
    for p in (4, 5):
        accumulate(mine[p])
    far(QUERY)
    accumulate(mine[7])
    for p in (4, 5, 7):
        from_sib(QUERY, p)
        accumulate(theirs[p])
    for h in range(HEADS_HERE):
        qrot[h] = rotate(qacc[:, h * HEAD : (h + 1) * HEAD]).astype(bf16)
    for p in range(8):
        from_sib(KEYS, p)

    ones = jnp.ones((BLOCK, HEAD), bf16)

    turns = (x, xm, xp, xo)

    def scores_of(h, block):
        rows = pl.ds(pl.multiple_of(block * BLOCK, BLOCK), BLOCK)
        return lax.dot_general(
            qrot[turns[h]], kv[0, rows], (((1,), (1,)), ((), ())), preferred_element_type=f32
        )

    def values_of(block):
        rows = pl.ds(pl.multiple_of(block * BLOCK, BLOCK), BLOCK)
        return jnp.concatenate([kv[1, rows], ones], axis=1)

    query_at = lax.broadcasted_iota(jnp.int32, (ROWS, BLOCK), 0) + core * ROWS
    allowed = lax.broadcasted_iota(jnp.int32, (ROWS, BLOCK), 1) <= query_at
    def hop(label, source, place, peer):
        copy = pltpu.make_async_remote_copy(
            src_ref=source, dst_ref=place, send_sem=rsend.at[label], recv_sem=rrecv.at[label],
            device_id=peer, device_id_type=MESH,
        )
        copy.start()
        started.append(copy)

    def landed(label, place):
        pltpu.make_async_remote_copy(
            src_ref=place, dst_ref=place, send_sem=rsend.at[label], recv_sem=rrecv.at[label],
            device_id=to_sib, device_id_type=MESH,
        ).wait_recv()

    def zplace(source, h, half=None):
        whole = heads.at[source, turns[h]]
        return whole if half is None else heads.at[source, turns[h], pl.ds(half * 128, 128)]

    def zsource(way, d):
        return lax.rem(z + 8 - d, 8) if way == 0 else lax.rem(z + d, 8)

    def zsend(h, way, d):
        place = zplace(zsource(way, d - 1), h, way if d == 4 else None)
        hop((h * 2 + way) * 4 + d - 1, place, place, (to_zp, to_zm)[way])

    def zland(h, way, d):
        landed((h * 2 + way) * 4 + d - 1, zplace(zsource(way, d), h, way if d == 4 else None))

    def zstep(first, d):
        for h in (first, first + 1):
            for way in range(2):
                zland(h, way, d)
                if d < 4:
                    zsend(h, way, d + 1)

    odd, doubles = lax.rem(chip, 2), lax.div(chip, 2)
    for pair_first in (0, 2):
        both = (pair_first, pair_first + 1)
        for h in both:
            scores = jnp.where(allowed, scores_of(h, chip), -1e30)
            high = jnp.max(scores, axis=1, keepdims=True)
            weights = jnp.exp2((scores - high) * SCORE_LOG2).astype(bf16)
            oacc[h] = jnp.dot(weights, values_of(chip), preferred_element_type=f32)
            macc[h] = jnp.broadcast_to(high, (ROWS, HEAD))

        def attend(first, width, both=both):
            blocks = range(width)
            values = [values_of(first + i) for i in blocks]
            for h in both:
                scores = [scores_of(h, first + i) for i in blocks]
                before = macc[h][:, :1]
                peak = scores[0]
                for more in scores[1:]:
                    peak = jnp.maximum(peak, more)
                high = jnp.maximum(before, jnp.max(peak, axis=1, keepdims=True))
                keep = jnp.exp2((before - high) * SCORE_LOG2)
                mixed = oacc[h] * keep
                for i in blocks:
                    weights = jnp.exp2((scores[i] - high) * SCORE_LOG2).astype(bf16)
                    mixed = mixed + jnp.dot(weights, values[i], preferred_element_type=f32)
                oacc[h] = mixed
                macc[h] = jnp.broadcast_to(high, (ROWS, HEAD))

        def attend_one(block, _):
            attend(block, 1)
            return 0

        def attend_two(i, _):
            attend(odd + 2 * i, 2)
            return 0

        lax.fori_loop(0, odd, attend_one, 0)
        lax.fori_loop(0, jnp.minimum(doubles, 2), attend_two, 0)
        if pair_first == 2:
            zstep(0, 1)
            near_x(OUTPUT)
            near_y(OUTPUT)
        lax.fori_loop(2, jnp.maximum(doubles, 2), attend_two, 0)
        for h in both:
            heads[z, turns[h]] = (oacc[h][:, :HEAD] / oacc[h][:, HEAD:]).astype(bf16)
            zsend(h, 0, 1)
            zsend(h, 1, 1)
    def columns_from(p, fresh, sides=(0, 1)):
        row, column = chips[p]
        place = row * 2 + column
        left = jnp.concatenate([heads[i, row] for i in range(8)], axis=1)
        for yi in sides:
            right = jnp.concatenate(
                [wo[place * 2 + i, yi].reshape(8 * HEAD, HEAD) for i in range(2)], axis=1
            )
            term = jnp.dot(left, right, preferred_element_type=f32)
            tacc[yi, column] = term if fresh else tacc[yi, column] + term

    zstep(0, 2)
    zstep(2, 1)
    opposite(OUTPUT)
    zstep(0, 3)
    zstep(2, 2)
    zstep(0, 4)
    zstep(2, 3)
    for p, fresh in ((0, True), (2, False), (1, True)):
        from_sib(OUTPUT, p)
        columns_from(p, fresh)
    zstep(2, 4)

    def hand_over(n, column):
        ysnd[column] = tacc[1 - yh, column].astype(bf16)
        hop(32 + n, ysnd.at[column], yrcv.at[column], to_yh)

    for p in (3, 6):
        from_sib(OUTPUT, p)
        columns_from(p, False)
    hand_over(0, yl)
    corners(OUTPUT)
    for p in (4, 5):
        from_sib(OUTPUT, p)
        columns_from(p, False)
    far(OUTPUT)
    from_sib(OUTPUT, 7)
    columns_from(7, False, (1 - yh,))
    hand_over(1, yp)
    columns_from(7, False, (yh,))
    for n, column in enumerate((yl, yp)):
        landed(32 + n, yrcv.at[column])
        at = pl.ds(pl.multiple_of(column * 256, 256), 256)
        wide = pl.ds(pl.multiple_of(w * BLOCK + column * 256, 256), 256)
        out_ref[:, at] = (hid[:, wide].astype(f32) + tacc[yh, column] + yrcv[column].astype(f32)).astype(bf16)
    for copy in started:
        copy.wait_send()


def local(hidden_states, norm_gain, query_weight, key_value_matrix, output_weight):
    tables = [jnp.asarray(t) for t in rope_constants()]
    anywhere = pl.BlockSpec(memory_space=pl.ANY)
    inside = pl.BlockSpec(memory_space=pltpu.VMEM)
    dma = pltpu.SemaphoreType.DMA
    return pl.pallas_call(
        body,
        out_shape=jax.ShapeDtypeStruct((ROWS, BLOCK), bf16),
        in_specs=[anywhere, inside, anywhere, anywhere, anywhere] + [anywhere] * 2,
        out_specs=inside,
        scratch_shapes=[
            pltpu.VMEM((2, ROWS, HEAD), f32),
            pltpu.VMEM((2, 1, HEAD), f32),
            pltpu.VMEM((ROWS, 8192), bf16),
            pltpu.VMEM((SHARDS, ROWS, BLOCK), bf16),
            pltpu.VMEM((SHARDS, BLOCK, HEAD), bf16),
            pltpu.VMEM((SHARDS, BLOCK, BLOCK), bf16),
            pltpu.VMEM((SHARDS, 2, 8, HEAD, HEAD), bf16),
            pltpu.VMEM((2, 8, HEAD, HEAD), bf16),
            pltpu.VMEM((2, SHARDS * ROWS, HEAD), bf16),
            pltpu.VMEM((ROWS, BLOCK), f32),
            pltpu.VMEM((HEADS_HERE, ROWS, HEAD), bf16),
            pltpu.VMEM((HEADS_HERE, ROWS, HEAD), f32),
            pltpu.VMEM((HEADS_HERE, ROWS, 2 * HEAD), f32),
            pltpu.VMEM((8, HEADS_HERE, ROWS, HEAD), bf16),
            pltpu.VMEM((2, 2, ROWS, 256), f32),
            pltpu.VMEM((2, ROWS, 256), bf16),
            pltpu.VMEM((2, ROWS, 256), bf16),
            dma((4, 18)),
            dma((4, 18)),
            dma((34,)),
            dma((34,)),
            dma((23,)),
            dma((23,)),
            dma((1,)),
            dma((1,)),
            dma((6,)),
        ],
        compiler_params=pltpu.CompilerParams(
            collective_id=0, has_side_effects=True, vmem_limit_bytes=56 * 1024 * 1024
        ),
    )(hidden_states, norm_gain, query_weight, key_value_matrix, output_weight, *tables)


def solution(mesh):
    in_specs = (P("seq", None), P(), P("seq", "wt"), P("seq", None), P("wt", "seq"))
    return jax.shard_map(local, mesh=mesh, in_specs=in_specs, out_specs=P("seq", "wt"), check_vma=False)
```
